256 devices in a mesh: row: 8 (over z), col: 32 (over y, x, core).
Axes of the slice: x: 4, y: 4, z: 8, core: 2. Of those that a mesh axis runs over, the one named last changes fastest.
Arguments:
- image_feats: bfloat16 [147456, 6144], P(('row', 'col')), may hold values from -24 to 24
- text_feats: bfloat16 [147456, 4096], P(('row', 'col')), may hold values from -24 to 24
- probe_image: bfloat16 [6144, 128], P('row'), may hold values from -0.078125 to 0.078125
- probe_text: bfloat16 [4096, 128], P('col'), may hold values from -0.09375 to 0.09375
Outputs:
- image_basis: float32 [6144, 128], P('row')
- text_basis: float32 [4096, 128], P('col')
The draws below stay inside these ranges and needn't reach their ends.
All inputs are finite; a program needn't handle non-finite values.
Results may differ from the reference program's by a relative error of at most 0.0031.
Values may be sent and summed in bfloat16 or wider, within the bound.
A program may use at most 64 MiB of HBM per device.

```python
import math
import jax
import jax.numpy as jnp
from jax import lax

DX = 6144
DY = 4096
RANK = 128
PAIRS = 147456


def raised(array, rng, source, target, parts, factor):
    def block_of(dim):
        return (jnp.arange(array.shape[dim]) // (array.shape[dim] // parts)).reshape((-1,) + (1,) * (array.ndim - 1 - dim))

    one_side = jax.random.permutation(rng, parts)[block_of(target)]
    second = (block_of(target) + parts // 2) % parts
    return jnp.where((block_of(source) == one_side) | (block_of(source) == second), factor * array, array)


def steps_of(own_key, shape, split, low, top_value):
    def one(dim, shards_of):
        steps = jax.random.uniform(jax.random.fold_in(jax.random.fold_in(own_key, 6), dim), (shards_of,), jnp.float32, low / len(split), top_value / len(split))
        return jnp.repeat(jnp.exp(steps), shape[dim] // shards_of).reshape((-1,) + (1,) * (len(shape) - dim - 1))

    factor_of = one(*split[0])
    for cut in split[1:]:
        factor_of = factor_of * one(*cut)
    return factor_of


def normal_values(own_key, shape, scale, bound, split=(), kind=jnp.bfloat16):
    drawn = scale * jax.random.normal(own_key, shape, jnp.float32)
    if split:
        drawn = drawn * steps_of(own_key, shape, split, -0.22, 0.18)
    return jnp.clip(drawn, -bound, bound).astype(kind)


def gaussian_with(rng, extent, deviation, most, split, heavy, held_as=jnp.bfloat16):
    values = deviation * jax.random.normal(rng, extent, jnp.float32)
    if split:
        values = values * steps_of(rng, extent, split, -0.22, 0.18)
    return jnp.clip(raised(values, jax.random.fold_in(rng, 3), *heavy), -most, most).astype(held_as)


def setup_inputs(seed: int = 0) -> dict:
    key_list = jax.random.split(jax.random.key(seed), 5)
    return {
        "image_feats": gaussian_with(key_list[0], (PAIRS, DX), 1.0, 24.0, ((0, 256),), (0, 1, 256, 6.0)),
        "text_feats": gaussian_with(key_list[1], (PAIRS, DY), 1.0, 24.0, ((0, 256),), (0, 1, 256, 6.0)),
        "probe_image": normal_values(key_list[2], (DX, RANK), DX ** -0.5, 0.078125, ((0, 8),)),
        "probe_text": normal_values(key_list[3], (DY, RANK), DY ** -0.5, 0.09375, ((0, 32),)),
    }


def orthonormal(panel, width):
    gram = jnp.dot(panel.T.astype(jnp.float32), panel.astype(jnp.float32), precision=lax.Precision.HIGHEST, preferred_element_type=jnp.float32)
    factor = jnp.linalg.cholesky(gram)
    basis = lax.linalg.triangular_solve(factor, panel, left_side=False, lower=True, transpose_a=True)
    return basis * math.sqrt(width)

def reference(image_feats, text_feats, probe_image, probe_text):
    sketch_text = jnp.dot(text_feats.astype(jnp.float32), probe_text.astype(jnp.float32), preferred_element_type=jnp.float32).astype(jnp.bfloat16)
    sketch_image = jnp.dot(image_feats.astype(jnp.float32), probe_image.astype(jnp.float32), preferred_element_type=jnp.float32).astype(jnp.bfloat16)
    dims = (((0,), (0,)), ((), ()))
    image_panel = lax.dot_general(image_feats.astype(jnp.float32), sketch_text.astype(jnp.float32), dims, preferred_element_type=jnp.float32)
    text_panel = lax.dot_general(text_feats.astype(jnp.float32), sketch_image.astype(jnp.float32), dims, preferred_element_type=jnp.float32)
    return (orthonormal(image_panel, DX), orthonormal(text_panel, DY))
```

```python
import functools
import math

import jax
import jax.numpy as jnp
from jax import lax
from jax.experimental import pallas as pl
from jax.experimental.pallas import tpu as pltpu
from jax.sharding import PartitionSpec as P

MESH = pl.DeviceIdType.MESH
F32 = jnp.float32
BF16 = jnp.bfloat16
HIGHEST = lax.Precision.HIGHEST

NZ = 8
NP = 16
SIDE = 4


def remote(src, dst, ssem, rsem, device):
    return pltpu.make_async_remote_copy(
        src_ref=src, dst_ref=dst, send_sem=ssem, recv_sem=rsem, device_id=device, device_id_type=MESH
    )


def drain(ref, sem):
    pltpu.make_async_copy(ref, ref, sem).wait()


def exchange(
    x_hbm, y_hbm, pi_ref, pt_ref,
    img_out, txt_out, gi_out, gt_out,
    X, Y, PT, PI, acc, St,
    JF, JS, JR, JP, RJ, ZS, ZR, FB, G, G2,
    TF, TS, TR, TP, RT, ZTS, ZTR, ZTF, ZTA,
    GIS, GIR, GIF, GIA, GTS, GTR, GTP, GTPR, GTF, GTA,
    lsem, ssem, rsem,
):
    z = lax.axis_index("row")
    col = lax.axis_index("col")
    p, c = col // 2, col % 2
    y, x = p // SIDE, p % SIDE
    sib = (z, p * 2 + (1 - c))
    pairs = X.shape[0]
    half = pi_ref.shape[0] // 2
    iblock = pi_ref.shape[0]

    def chip(k):
        return ((y + k // SIDE) % SIDE) * SIDE + (x + k % SIDE) % SIDE

    def plane_dev(k):
        return (z, chip(k) * 2 + c)

    def z_dev(d):
        return ((z + d) % NZ, col)

    load_y = pltpu.make_async_copy(y_hbm, Y, lsem.at[0])
    load_x = pltpu.make_async_copy(x_hbm, X, lsem.at[1])
    load_y.start()
    load_x.start()

    barrier = pltpu.get_barrier_semaphore()

    def greet_plane(k, _):
        pl.semaphore_signal(barrier, inc=1, device_id=plane_dev(k), device_id_type=MESH)
        return 0

    def greet_z(d, _):
        pl.semaphore_signal(barrier, inc=1, device_id=z_dev(d), device_id_type=MESH)
        return 0

    lax.fori_loop(1, NZ, greet_z, 0)
    lax.fori_loop(1, NP, greet_plane, 0)
    pl.semaphore_signal(barrier, inc=1, device_id=sib, device_id_type=MESH)
    pl.semaphore_wait(barrier, NZ - 1 + NP - 1 + 1)

    def to_plane(i, src, dst):
        def body(k, _):
            remote(src(k), dst(k), ssem.at[i], rsem.at[i], plane_dev(k)).start()
            return 0

        lax.fori_loop(1, NP, body, 0)

    def to_z(i, src, dst):
        def body(d, _):
            remote(src(d), dst(d), ssem.at[i], rsem.at[i], z_dev(d)).start()
            return 0

        lax.fori_loop(1, NZ, body, 0)

    mine = pi_ref.at[pl.ds(pl.multiple_of(c * half, half), half)]
    to_z(1, lambda d: mine, lambda d: PI.at[z, c])
    to_plane(0, lambda k: pt_ref, lambda k: PT.at[p, c])
    PT[p, c] = pt_ref[...]
    PI[z, c] = pi_ref[pl.ds(pl.multiple_of(c * half, half), half), :]
    drain(PT.at[pl.ds(0, NP - 1), 0], rsem.at[0])
    remote(PT.at[:, c], PT.at[:, c], ssem.at[2], rsem.at[2], sib).start()
    load_y.wait()
    drain(PT.at[:, 0], rsem.at[2])

    acc[...] = jnp.zeros_like(acc)

    def text_sketch(i, _):
        cols = pl.ds(pl.multiple_of(i * 1024, 1024), 1024)
        acc[...] += jnp.dot(
            Y[:, cols], PT[pl.ds(i * 4, 4)].reshape(1024, 128), preferred_element_type=F32
        )
        return 0

    lax.fori_loop(0, NP // 4, text_sketch, 0)
    St[...] = acc[...].T.astype(BF16)
    load_x.wait()

    def image_panel(q, _):
        parts = []
        for e in range(2):
            cols = pl.ds(pl.multiple_of((q * 2 + e) * iblock, iblock), iblock)
            parts.append(jnp.dot(St[...], X[:, cols], preferred_element_type=F32))
        for h in range(2):
            both = jnp.concatenate(
                [d[:, h * half:(h + 1) * half].reshape(NP, 8, half) for d in parts], axis=1
            )
            JF[h, q] = both
            JS[h, q] = both.astype(BF16)
        remote(JS.at[1 - c, q], JR.at[q], ssem.at[3], rsem.at[3], sib).start()
        return 0

    lax.fori_loop(0, NZ // 2, image_panel, 0)
    drain(JR, rsem.at[3])

    def image_pair(q, _):
        JP[q] = (JF[c, q] + JR[q].astype(F32)).astype(BF16)
        return 0

    lax.fori_loop(0, NZ // 2, image_pair, 0)
    to_plane(4, lambda k: JP.at[:, chip(k)], lambda k: RJ.at[k - 1])

    drain(PI.at[pl.ds(0, NZ - 1), 0], rsem.at[1])
    remote(PI.at[:, c], PI.at[:, c], ssem.at[5], rsem.at[5], sib).start()
    drain(PI.at[:, 0], rsem.at[5])
    acc[...] = jnp.zeros_like(acc)

    def image_sketch(i, _):
        cols = pl.ds(pl.multiple_of(i * iblock, iblock), iblock)
        acc[...] += jnp.dot(
            X[:, cols], PI[i].reshape(iblock, 128), preferred_element_type=F32
        )
        return 0

    lax.fori_loop(0, NZ, image_sketch, 0)
    St[...] = acc[...].T.astype(BF16)

    def text_panel(q, _):
        d = jnp.dot(
            St[...], Y[:, pl.ds(pl.multiple_of(q * 1024, 1024), 1024)], preferred_element_type=F32
        )
        for i in range(4):
            for h in range(2):
                one = d[:, (2 * i + h) * 128:(2 * i + h + 1) * 128]
                TF[h, q * 4 + i] = one
                TS[h, q * 4 + i] = one.astype(BF16)
        rows = pl.ds(q * 4, 4)
        remote(TS.at[1 - c, rows], TR.at[rows], ssem.at[6], rsem.at[6], sib).start()
        return 0

    lax.fori_loop(0, NP // 4, text_panel, 0)
    drain(TR, rsem.at[6])

    def text_pair(q, _):
        TP[q] = (TF[c, q] + TR[q].astype(F32)).astype(BF16)
        return 0

    lax.fori_loop(0, NP, text_pair, 0)
    to_plane(7, lambda k: TP.at[chip(k)], lambda k: RT.at[k - 1])

    drain(RJ, rsem.at[4])
    own = JF[c, :, p] + JR[:, p].astype(F32)
    own = lax.fori_loop(0, NP - 1, lambda k, a: a + RJ[k].astype(F32), own)
    ZS[...] = own.reshape(NZ, 8, half)
    to_z(8, lambda d: ZS.at[(z + d) % NZ], lambda d: ZR.at[d - 1])
    drain(ZR, rsem.at[8])
    FB[...] = lax.fori_loop(0, NZ - 1, lambda k, a: a + ZR[k], ZS[z])
    to_plane(9, lambda k: FB, lambda k: G.at[p])
    G[p] = FB[...]

    drain(RT, rsem.at[7])
    town = TF[c, p] + TR[p].astype(F32)
    town = lax.fori_loop(0, NP - 1, lambda k, a: a + RT[k].astype(F32), town)
    ZTS[...] = town.reshape(NZ, 16, 128)
    to_z(10, lambda d: ZTS.at[(z + d) % NZ], lambda d: ZTR.at[d - 1])

    drain(G.at[pl.ds(0, NP - 1)], rsem.at[9])
    remote(G, G2, ssem.at[11], rsem.at[11], sib).start()
    img_out[:, pl.ds(pl.multiple_of(c * half, half), half)] = G[...].reshape(128, half)
    drain(G2, rsem.at[11])
    img_out[:, pl.ds(pl.multiple_of((1 - c) * half, half), half)] = G2[...].reshape(128, half)
    full = img_out[...]
    nt = (((1,), (1,)), ((), ()))
    gram = lax.dot_general(full, full, nt, precision=HIGHEST, preferred_element_type=F32)
    GIS[...] = gram.reshape(NZ, 16, 128)
    to_z(12, lambda d: GIS.at[(z + d) % NZ], lambda d: GIR.at[d - 1])

    drain(ZTR, rsem.at[10])
    ZTF[...] = lax.fori_loop(0, NZ - 1, lambda k, a: a + ZTR[k], ZTS[z])
    to_z(13, lambda d: ZTF, lambda d: ZTA.at[z])
    ZTA[z] = ZTF[...]

    drain(GIR, rsem.at[12])
    GIF[...] = lax.fori_loop(0, NZ - 1, lambda k, a: a + GIR[k], GIS[z])
    to_z(14, lambda d: GIF, lambda d: GIA.at[z])
    GIA[z] = GIF[...]

    drain(ZTA.at[pl.ds(0, NZ - 1)], rsem.at[13])
    block = ZTA[...].reshape(128, 128)
    txt_out[...] = block
    GTS[...] = lax.dot_general(block, block, nt, precision=HIGHEST, preferred_element_type=F32)
    remote(GTS, GTR, ssem.at[15], rsem.at[15], sib).start()
    drain(GTR, rsem.at[15])
    GTP[...] = (GTS[...] + GTR[...]).reshape(NP, 8, 128)
    to_plane(16, lambda k: GTP.at[chip(k)], lambda k: GTPR.at[k - 1])
    drain(GTPR, rsem.at[16])
    GTF[...] = lax.fori_loop(0, NP - 1, lambda k, a: a + GTPR[k], GTP[p])
    to_plane(17, lambda k: GTF, lambda k: GTA.at[p])
    GTA[p] = GTF[...]

    drain(GIA.at[pl.ds(0, NZ - 1)], rsem.at[14])
    gi_out[...] = GIA[...].reshape(128, 128)
    drain(GTA.at[pl.ds(0, NP - 1)], rsem.at[17])
    gt_out[...] = GTA[...].reshape(128, 128)

    drain(PT.at[pl.ds(0, NP - 1), 0], ssem.at[0])
    drain(PI.at[pl.ds(0, NZ - 1), 0], ssem.at[1])
    drain(PT.at[:, 0], ssem.at[2])
    drain(JR, ssem.at[3])
    drain(RJ, ssem.at[4])
    drain(PI.at[:, 0], ssem.at[5])
    drain(TR, ssem.at[6])
    drain(RT, ssem.at[7])
    drain(ZR, ssem.at[8])
    drain(G.at[pl.ds(0, NP - 1)], ssem.at[9])
    drain(ZTR, ssem.at[10])
    drain(G2, ssem.at[11])
    drain(GIR, ssem.at[12])
    drain(ZTA.at[pl.ds(0, NZ - 1)], ssem.at[13])
    drain(GIA.at[pl.ds(0, NZ - 1)], ssem.at[14])
    drain(GTR, ssem.at[15])
    drain(GTPR, ssem.at[16])
    drain(GTA.at[pl.ds(0, NP - 1)], ssem.at[17])


def run_exchange(x, y, pi, pt):
    pairs, dx = x.shape
    dy = y.shape[1]
    rank = 128
    iblock = dx // NZ
    half = iblock // 2
    quads = NZ // 2
    vm = pltpu.VMEM
    scratch = [
        vm((pairs, dx), BF16), vm((pairs, dy), BF16),
        vm((NP, 2, 128, rank), BF16), vm((NZ, 2, half, rank), BF16),
        vm((pairs, rank), F32), vm((rank, pairs), BF16),
        vm((2, quads, NP, 16, half), F32), vm((2, quads, NP, 16, half), BF16),
        vm((quads, NP, 16, half), BF16), vm((quads, NP, 16, half), BF16),
        vm((NP - 1, quads, 16, half), BF16),
        vm((NZ, 8, half), F32), vm((NZ - 1, 8, half), F32), vm((8, half), F32),
        vm((NP, 8, half), F32), vm((NP, 8, half), F32),
        vm((2, NP, rank, 128), F32), vm((2, NP, rank, 128), BF16),
        vm((NP, rank, 128), BF16), vm((NP, rank, 128), BF16),
        vm((NP - 1, rank, 128), BF16),
        vm((NZ, 16, 128), F32), vm((NZ - 1, 16, 128), F32), vm((16, 128), F32), vm((NZ, 16, 128), F32),
        vm((NZ, 16, 128), F32), vm((NZ - 1, 16, 128), F32), vm((16, 128), F32), vm((NZ, 16, 128), F32),
        vm((128, 128), F32), vm((128, 128), F32),
        vm((NP, 8, 128), F32), vm((NP - 1, 8, 128), F32), vm((8, 128), F32), vm((NP, 8, 128), F32),
        pltpu.SemaphoreType.DMA((2,)), pltpu.SemaphoreType.DMA((18,)), pltpu.SemaphoreType.DMA((18,)),
    ]
    vspec = pl.BlockSpec(memory_space=pltpu.VMEM)
    aspec = pl.BlockSpec(memory_space=pl.ANY)
    square = jax.ShapeDtypeStruct((rank, rank), F32)
    return pl.pallas_call(
        exchange,
        out_shape=(jax.ShapeDtypeStruct((rank, iblock), F32), square, square, square),
        in_specs=[aspec, aspec, vspec, vspec],
        out_specs=(vspec,) * 4,
        scratch_shapes=scratch,
        name="panels",
        compiler_params=pltpu.CompilerParams(
            collective_id=0, has_side_effects=True, vmem_limit_bytes=48 << 20
        ),
        cost_estimate=pl.CostEstimate(
            flops=4 * pairs * (dx + dy) * rank, bytes_accessed=2 * pairs * (dx + dy), transcendentals=0
        ),
    )(x, y, pi, pt)


def lower_inverse(gram):
    n = gram.shape[0]
    lane = lax.broadcasted_iota(jnp.int32, (n, n), 1)
    sub = lax.broadcasted_iota(jnp.int32, (n, n), 0)
    w = gram
    scale = jnp.zeros((n, 1), F32)
    rows = lax.broadcasted_iota(jnp.int32, (n, 1), 0)
    for j in range(n):
        row = jnp.where(lane[:1] == j, 1.0, w[j:j + 1, :])
        column = w[:, j:j + 1]
        pivot = column[j:j + 1, :]
        inv = 1.0 / pivot
        f = jnp.where(rows > j, column * inv, 0.0)
        w = jnp.where((lane == j) & (sub >= j), jnp.where(sub == j, 1.0, 0.0), w) - f * row
        scale = jnp.where(rows == j, lax.rsqrt(pivot), scale)
    return jnp.where(lane <= sub, w, 0.0) * scale


def finish_kernel(img_ref, txt_ref, gi_ref, gt_ref, img_out, txt_out, *, image_width, text_width):
    tt = (((0,), (1,)), ((), ()))
    li = lower_inverse(gi_ref[...]) * math.sqrt(image_width)
    img_out[...] = lax.dot_general(img_ref[...], li, tt, precision=HIGHEST, preferred_element_type=F32)
    lt = lower_inverse(gt_ref[...]) * math.sqrt(text_width)
    txt_out[...] = lax.dot_general(txt_ref[...], lt, tt, precision=HIGHEST, preferred_element_type=F32)


def finish(img, txt, gi, gt, image_width, text_width):
    vspec = pl.BlockSpec(memory_space=pltpu.VMEM)
    return pl.pallas_call(
        functools.partial(finish_kernel, image_width=image_width, text_width=text_width),
        out_shape=(
            jax.ShapeDtypeStruct((img.shape[1], 128), F32),
            jax.ShapeDtypeStruct((txt.shape[1], 128), F32),
        ),
        in_specs=[vspec] * 4,
        out_specs=(vspec, vspec),
        name="bases",
        compiler_params=pltpu.CompilerParams(vmem_limit_bytes=32 << 20),
    )(img, txt, gi, gt)


def per_device(image_feats, text_feats, probe_image, probe_text):
    img, txt, gi, gt = run_exchange(image_feats, text_feats, probe_image, probe_text)
    return finish(img, txt, gi, gt, image_feats.shape[1], text_feats.shape[1])


def solution(mesh):
    in_specs = (P(("row", "col"), None), P(("row", "col"), None), P("row", None), P("col", None))
    out_specs = (P("row", None), P("col", None))
    return jax.shard_map(
        per_device, mesh=mesh, in_specs=in_specs, out_specs=out_specs, check_vma=False
    )
```

```python
import functools
import math

import jax
import jax.numpy as jnp
from jax import lax
from jax.experimental import pallas as pl
from jax.experimental.pallas import tpu as pltpu
from jax.sharding import PartitionSpec as P

MESH = pl.DeviceIdType.MESH
F32 = jnp.float32
BF16 = jnp.bfloat16
HIGHEST = lax.Precision.HIGHEST

NZ = 8
NP = 16
SIDE = 4
QUADS = NZ // 2


def remote(src, dst, ssem, rsem, device):
    return pltpu.make_async_remote_copy(
        src_ref=src, dst_ref=dst, send_sem=ssem, recv_sem=rsem, device_id=device, device_id_type=MESH
    )


def drain(ref, sem):
    pltpu.make_async_copy(ref, ref, sem).wait()


def exchange(
    x_hbm, y_hbm, pi_hbm, pt_hbm,
    img_out, txt_out, gi_out, gt_out,
    X, Y, pi_ref, pt_ref, PT, PI, acc, St,
    JF, JS, JR, JP, RJ, ZS, ZR, FB, G, G2,
    TF, TR, TP, RT, ZT,
    GI, GTS, GTR, GTA,
    lsem, ssem, rsem,
):
    z = lax.axis_index("row")
    col = lax.axis_index("col")
    p, c = col // 2, col % 2
    y, x = p // SIDE, p % SIDE
    sib = (z, p * 2 + (1 - c))
    iblock = pi_ref.shape[0]
    half = iblock // 2
    near = half - NP * 16
    nt = (((1,), (1,)), ((), ()))

    def chip(k):
        return ((y + k // SIDE) % SIDE) * SIDE + (x + k % SIDE) % SIDE

    def plane_dev(k):
        return (z, chip(k) * 2 + c)

    def z_dev(d):
        return ((z + d) % NZ, col)

    load_t = pltpu.make_async_copy(pt_hbm, pt_ref, lsem.at[2])
    load_i = pltpu.make_async_copy(pi_hbm, pi_ref, lsem.at[3])
    load_t.start()
    load_i.start()
    load_y = pltpu.make_async_copy(y_hbm, Y, lsem.at[0])
    load_x = pltpu.make_async_copy(x_hbm, X, lsem.at[1])
    load_y.start()
    load_x.start()

    barrier = pltpu.get_barrier_semaphore()

    def greet_plane(k, _):
        pl.semaphore_signal(barrier, inc=1, device_id=plane_dev(k), device_id_type=MESH)
        return 0

    def greet_z(d, _):
        pl.semaphore_signal(barrier, inc=1, device_id=z_dev(d), device_id_type=MESH)
        return 0

    lax.fori_loop(1, NZ, greet_z, 0)
    lax.fori_loop(1, NP, greet_plane, 0)
    pl.semaphore_signal(barrier, inc=1, device_id=sib, device_id_type=MESH)
    load_t.wait()
    load_i.wait()
    pl.semaphore_wait(barrier, NZ - 1 + NP - 1 + 1)

    def to_plane(i, src, dst):
        def body(k, _):
            remote(src(k), dst(k), ssem.at[i], rsem.at[i], plane_dev(k)).start()
            return 0

        lax.fori_loop(1, NP, body, 0)

    def to_z(i, src, dst):
        def body(d, _):
            remote(src(d), dst(d), ssem.at[i], rsem.at[i], z_dev(d)).start()
            return 0

        lax.fori_loop(1, NZ, body, 0)

    first = pl.ds(pl.multiple_of(c * half, 16), near)
    share = pl.ds(pl.multiple_of(c * half + near + 16 * p, 16), 16)
    slot = pl.ds(pl.multiple_of(near + 16 * p, 16), 16)
    to_z(1, lambda d: pi_ref.at[share], lambda d: PI.at[z, c, slot])
    to_plane(0, lambda k: pt_ref, lambda k: PT.at[p, c])
    to_z(4, lambda d: pi_ref.at[first], lambda d: PI.at[z, c, pl.ds(0, near)])
    PT[p, c] = pt_ref[...]
    PI[z, c, pl.ds(0, near), :] = pi_ref[first, :]
    PI[z, c, slot, :] = pi_ref[share, :]
    small = PI.at[pl.ds(0, NZ - 1), 0, pl.ds(0, 16)]
    straight = PI.at[pl.ds(0, NZ - 1), 0, pl.ds(0, near)]
    spread = PI.at[:, 0, pl.ds(0, 16 * (NP - 1))]
    drain(small, rsem.at[1])
    to_plane(3, lambda k: PI.at[:, c, slot], lambda k: PI.at[:, c, slot])
    drain(PT.at[pl.ds(0, NP - 1), 0], rsem.at[0])
    remote(PT.at[:, c], PT.at[:, c], ssem.at[2], rsem.at[2], sib).start()
    load_y.wait()
    acc[...] = jnp.zeros_like(acc)
    drain(PT.at[:, 0], rsem.at[2])

    def text_sketch(i, _):
        cols = pl.ds(pl.multiple_of(i * 1024, 1024), 1024)
        acc[...] += jnp.dot(
            Y[:, cols], PT[pl.ds(i * 4, 4)].reshape(1024, 128), preferred_element_type=F32
        )
        return 0

    lax.fori_loop(0, NP // 4, text_sketch, 0)
    St[...] = acc[...].T.astype(BF16)
    load_x.wait()

    def pair(i):
        return (z // 2 + 1 + i) % QUADS

    def image_panel(i, _):
        @pl.when(i < QUADS)
        def _():
            q = pair(i)
            parts = []
            for e in range(2):
                cols = pl.ds(pl.multiple_of((q * 2 + e) * iblock, iblock), iblock)
                parts.append(jnp.dot(St[...], X[:, cols], preferred_element_type=F32))
            for h in range(2):
                both = jnp.concatenate(
                    [d[:, h * half:(h + 1) * half].reshape(NP, 8, half) for d in parts], axis=1
                )
                JF[h, q] = both
                JS[h, q] = both.astype(BF16)
            remote(JS.at[1 - c, q], JR.at[q], ssem.at[16 + q], rsem.at[16 + q], sib).start()

        @pl.when(i > 0)
        def _():
            q = pair(i - 1)
            drain(JR.at[q], rsem.at[16 + q])
            JP[q] = (JF[c, q] + JR[q].astype(F32)).astype(BF16)
            to_plane(20 + q, lambda k: JP.at[q, chip(k)], lambda k: RJ.at[q, k - 1])

        return 0

    lax.fori_loop(0, QUADS + 1, image_panel, 0)

    acc[...] = jnp.zeros_like(acc)
    drain(straight, rsem.at[4])
    drain(spread, rsem.at[3])
    remote(PI.at[:, c], PI.at[:, c], ssem.at[5], rsem.at[5], sib).start()
    drain(PI.at[:, 0], rsem.at[5])

    def image_sketch(i, _):
        cols = pl.ds(pl.multiple_of(i * iblock, iblock), iblock)
        acc[...] += jnp.dot(
            X[:, cols], PI[i].reshape(iblock, 128), preferred_element_type=F32
        )
        return 0

    lax.fori_loop(0, NZ, image_sketch, 0)
    St[...] = acc[...].T.astype(BF16)

    def quarter(i):
        return (y + 1 + i) % SIDE

    def text_panel(i, _):
        @pl.when(i < SIDE)
        def _():
            r = quarter(i)
            d = jnp.dot(
                St[...], Y[:, pl.ds(pl.multiple_of(r * 1024, 1024), 1024)],
                preferred_element_type=F32,
            )
            for j in range(4):
                for h in range(2):
                    TF[h, r * 4 + j] = d[:, (2 * j + h) * 128:(2 * j + h + 1) * 128]
            rows = pl.ds(r * 4, 4)
            remote(
                TF.at[1 - c, rows], TR.at[rows], ssem.at[24 + r], rsem.at[24 + r], sib
            ).start()

        @pl.when(i > 0)
        def _():
            r = quarter(i - 1)
            rows = pl.ds(r * 4, 4)
            drain(TR.at[rows], rsem.at[24 + r])
            TP[rows] = (TF[c, rows] + TR[rows]).astype(BF16)

            def body(k, _):
                remote(
                    TP.at[chip(k)], RT.at[k - 1], ssem.at[7], rsem.at[7], plane_dev(k)
                ).start()
                return 0

            dy = (r - y + SIDE) % SIDE
            lax.fori_loop(jnp.where(dy == 0, 1, dy * SIDE), dy * SIDE + SIDE, body, 0)

        return 0

    lax.fori_loop(0, SIDE + 1, text_panel, 0)

    def image_sum(i, _):
        q = pair(i)
        drain(RJ.at[q], rsem.at[20 + q])
        own = JF[c, q, p] + JR[q, p].astype(F32)
        own = lax.fori_loop(0, NP - 1, lambda k, a: a + RJ[q, k].astype(F32), own)
        ZS[pl.ds(q * 2, 2)] = own.reshape(2, 8, half)
        return 0

    lax.fori_loop(0, QUADS, image_sum, 0)
    to_z(8, lambda d: ZS.at[(z + d) % NZ], lambda d: ZR.at[d - 1])

    drain(RT, rsem.at[7])
    town = TF[c, p] + TR[p]
    town = lax.fori_loop(0, NP - 1, lambda k, a: a + RT[k].astype(F32), town)
    ZT[z] = town.astype(BF16)
    to_z(10, lambda d: ZT.at[z], lambda d: ZT.at[z])

    drain(ZR, rsem.at[8])
    FB[...] = lax.fori_loop(0, NZ - 1, lambda k, a: a + ZR[k], ZS[z])
    to_plane(9, lambda k: FB, lambda k: G.at[p])
    G[p] = FB[...]

    drain(ZT.at[pl.ds(0, NZ - 1)], rsem.at[10])
    block = lax.fori_loop(
        1, NZ, lambda k, a: a + ZT[k].astype(F32), ZT[0].astype(F32)
    )
    txt_out[...] = block.T
    GTS[...] = lax.dot_general(
        block, block, nt, precision=HIGHEST, preferred_element_type=F32
    ).reshape(2, 64, 128)
    remote(GTS.at[1 - c], GTR, ssem.at[15], rsem.at[15], sib).start()

    drain(G.at[pl.ds(0, NP - 1)], rsem.at[9])
    remote(G, G2, ssem.at[11], rsem.at[11], sib).start()

    drain(GTR, rsem.at[15])
    GTA[p] = GTS[c] + GTR[...]
    to_plane(6, lambda k: GTA.at[p], lambda k: GTA.at[p])

    drain(G2, rsem.at[11])
    lo = pl.ds(pl.multiple_of(c * half, 128), half)
    hi = pl.ds(pl.multiple_of((1 - c) * half, 128), half)
    img_out[lo, :] = G[...].reshape(128, half).T
    img_out[hi, :] = G2[...].reshape(128, half).T
    full = img_out[...]
    tn = (((0,), (0,)), ((), ()))
    gram = lax.dot_general(full, full, tn, precision=HIGHEST, preferred_element_type=F32)
    GI[z] = jnp.where(c == 0, gram[:64], gram[64:])
    to_z(12, lambda d: GI.at[z], lambda d: GI.at[z])

    drain(GI.at[pl.ds(0, NZ - 1)], rsem.at[12])
    mine = pl.ds(pl.multiple_of(c * 64, 64), 64)
    gi_out[mine, :] = lax.fori_loop(1, NZ, lambda k, a: a + GI[k], GI[0])
    remote(gi_out.at[mine], gi_out.at[mine], ssem.at[13], rsem.at[13], sib).start()
    drain(GTA.at[pl.ds(0, NP - 1)], rsem.at[6])
    gt_out[mine, :] = lax.fori_loop(1, NP, lambda k, a: a + GTA[k], GTA[0])
    remote(gt_out.at[mine], gt_out.at[mine], ssem.at[14], rsem.at[14], sib).start()
    drain(gi_out.at[pl.ds(0, 64)], rsem.at[13])
    drain(gt_out.at[pl.ds(0, 64)], rsem.at[14])

    drain(PT.at[pl.ds(0, NP - 1), 0], ssem.at[0])
    drain(small, ssem.at[1])
    drain(PT.at[:, 0], ssem.at[2])
    drain(spread, ssem.at[3])
    drain(straight, ssem.at[4])
    drain(PI.at[:, 0], ssem.at[5])
    drain(GTA.at[pl.ds(0, NP - 1)], ssem.at[6])
    drain(RT, ssem.at[7])
    drain(ZR, ssem.at[8])
    drain(G.at[pl.ds(0, NP - 1)], ssem.at[9])
    drain(ZT.at[pl.ds(0, NZ - 1)], ssem.at[10])
    drain(G2, ssem.at[11])
    drain(GI.at[pl.ds(0, NZ - 1)], ssem.at[12])
    drain(gi_out.at[pl.ds(0, 64)], ssem.at[13])
    drain(gt_out.at[pl.ds(0, 64)], ssem.at[14])
    drain(GTR, ssem.at[15])

    def left(q, _):
        drain(JR.at[q], ssem.at[16 + q])
        drain(RJ.at[q], ssem.at[20 + q])
        drain(TR.at[pl.ds(q * 4, 4)], ssem.at[24 + q])
        return 0

    lax.fori_loop(0, QUADS, left, 0)


def run_exchange(x, y, pi, pt):
    pairs, dx = x.shape
    dy = y.shape[1]
    rank = 128
    iblock = dx // NZ
    half = iblock // 2
    vm = pltpu.VMEM
    scratch = [
        vm((pairs, dx), BF16), vm((pairs, dy), BF16),
        vm((iblock, rank), BF16), vm((128, rank), BF16),
        vm((NP, 2, 128, rank), BF16), vm((NZ, 2, half, rank), BF16),
        vm((pairs, rank), F32), vm((rank, pairs), BF16),
        vm((2, QUADS, NP, 16, half), F32), vm((2, QUADS, NP, 16, half), BF16),
        vm((QUADS, NP, 16, half), BF16), vm((QUADS, NP, 16, half), BF16),
        vm((QUADS, NP - 1, 16, half), BF16),
        vm((NZ, 8, half), F32), vm((NZ - 1, 8, half), F32), vm((8, half), F32),
        vm((NP, 8, half), F32), vm((NP, 8, half), F32),
        vm((2, NP, rank, 128), F32), vm((NP, rank, 128), F32),
        vm((NP, rank, 128), BF16), vm((NP - 1, rank, 128), BF16),
        vm((NZ, rank, 128), BF16),
        vm((NZ, 64, 128), F32), vm((2, 64, 128), F32), vm((64, 128), F32),
        vm((NP, 64, 128), F32),
        pltpu.SemaphoreType.DMA((4,)), pltpu.SemaphoreType.DMA((28,)), pltpu.SemaphoreType.DMA((28,)),
    ]
    vspec = pl.BlockSpec(memory_space=pltpu.VMEM)
    aspec = pl.BlockSpec(memory_space=pl.ANY)
    square = jax.ShapeDtypeStruct((rank, rank), F32)
    return pl.pallas_call(
        exchange,
        out_shape=(jax.ShapeDtypeStruct((iblock, rank), F32), square, square, square),
        in_specs=[aspec] * 4,
        out_specs=(vspec,) * 4,
        scratch_shapes=scratch,
        name="panels",
        compiler_params=pltpu.CompilerParams(
            collective_id=0, has_side_effects=True, vmem_limit_bytes=60 << 20
        ),
        cost_estimate=pl.CostEstimate(
            flops=4 * pairs * (dx + dy) * rank, bytes_accessed=2 * pairs * (dx + dy), transcendentals=0
        ),
    )(x, y, pi, pt)


def lower_inverses(grams, outer=32):
    n = grams[0].shape[0]
    m = len(grams)
    lane8 = lax.broadcasted_iota(jnp.int32, (8, n), 1)
    sub8 = lax.broadcasted_iota(jnp.int32, (8, n), 0)
    lane = lax.broadcasted_iota(jnp.int32, (n, n), 1)
    laneo = lax.broadcasted_iota(jnp.int32, (outer, n), 1)
    subo = lax.broadcasted_iota(jnp.int32, (outer, n), 0)
    nv = outer // 8
    work = list(grams)
    done = [[] for _ in range(m)]
    for b in range(n // outer):
        j0 = b * outer
        R = [[w[j0 + 8 * v:j0 + 8 * v + 8, :] for v in range(nv)] for w in work]
        rec = [[None] * nv for _ in range(m)]
        scl = [[None] * nv for _ in range(m)]
        for s in range(nv):
            cols = [[[jnp.broadcast_to(R[t][v][:, j0 + 8 * s + k:j0 + 8 * s + k + 1], (8, n)) for v in range(nv)] if True else None
                     for k in range(8)] for t in range(m)]
            for t in range(m):
                rec[t][s] = jnp.zeros((8, n), F32); scl[t][s] = jnp.zeros((8, n), F32)
            for k in range(8):
                j = j0 + 8 * s + k
                for t in range(m):
                    piv = jnp.broadcast_to(cols[t][k][s][k:k + 1, :], (8, n))
                    inv = 1.0 / piv
                    rec[t][s] = jnp.where(sub8 == k, inv, rec[t][s])
                    scl[t][s] = jnp.where(sub8 == k, lax.rsqrt(piv), scl[t][s])
                    prow = jnp.where(lane8 == j, 1.0, jnp.broadcast_to(R[t][s][k:k + 1, :], (8, n)))
                    nxt = {q: jnp.broadcast_to(cols[t][q][s][k:k + 1, :], (8, n)) for q in range(k + 1, 8)}
                    for v in range(s, nv):
                        f = cols[t][k][v] * inv
                        hit = lane8 == j
                        if v == s:
                            f = jnp.where(sub8 > k, f, 0.0)
                            hit = hit & (sub8 >= k)
                            base = jnp.where(hit, jnp.where(sub8 == k, 1.0, 0.0), R[t][v])
                        else:
                            base = jnp.where(hit, 0.0, R[t][v])
                        R[t][v] = base - f * prow
                        for q in range(k + 1, 8):
                            cols[t][q][v] = cols[t][q][v] - f * nxt[q]
        for t in range(m):
            rows = jnp.concatenate(R[t], axis=0)
            inv = jnp.concatenate(rec[t], axis=0)
            scale = jnp.concatenate(scl[t], axis=0)
            done[t].append(jnp.where(laneo <= subo + j0, rows * scale, 0.0))
            if j0 + outer < n:
                right = laneo >= j0 + outer
                fac = jnp.where(right, rows * inv, 0.0)
                keep = jnp.where(right | (laneo <= subo + j0), rows, 0.0)
                upd = lax.dot_general(fac, keep, (((0,), (0,)), ((), ())), precision=HIGHEST, preferred_element_type=F32)
                work[t] = jnp.where((lane >= j0) & (lane < j0 + outer), 0.0, work[t]) - upd
    return [jnp.concatenate(d, axis=0) for d in done]

def finish_kernel(
    img_hbm, txt_hbm, gi_ref, gt_ref, img_out, txt_out, img, txt, sem, *, image_width, text_width
):
    load_i = pltpu.make_async_copy(img_hbm, img, sem.at[0])
    load_t = pltpu.make_async_copy(txt_hbm, txt, sem.at[1])
    load_i.start()
    load_t.start()
    li, lt = lower_inverses([gi_ref[...], gt_ref[...]])
    nt = (((1,), (1,)), ((), ()))
    load_i.wait()
    load_t.wait()
    img_out[...] = lax.dot_general(
        img[...], li * math.sqrt(image_width), nt, precision=HIGHEST, preferred_element_type=F32
    )
    txt_out[...] = lax.dot_general(
        txt[...], lt * math.sqrt(text_width), nt, precision=HIGHEST, preferred_element_type=F32
    )


def finish(img, txt, gi, gt, image_width, text_width):
    vspec = pl.BlockSpec(memory_space=pltpu.VMEM)
    aspec = pl.BlockSpec(memory_space=pl.ANY)
    return pl.pallas_call(
        functools.partial(finish_kernel, image_width=image_width, text_width=text_width),
        out_shape=(jax.ShapeDtypeStruct(img.shape, F32), jax.ShapeDtypeStruct(txt.shape, F32)),
        in_specs=[aspec, aspec, vspec, vspec],
        out_specs=(vspec, vspec),
        scratch_shapes=[
            pltpu.VMEM(img.shape, F32), pltpu.VMEM(txt.shape, F32), pltpu.SemaphoreType.DMA((2,))
        ],
        name="bases",
        compiler_params=pltpu.CompilerParams(vmem_limit_bytes=60 << 20),
    )(img, txt, gi, gt)


def per_device(image_feats, text_feats, probe_image, probe_text):
    img, txt, gi, gt = run_exchange(image_feats, text_feats, probe_image, probe_text)
    return finish(img, txt, gi, gt, image_feats.shape[1], text_feats.shape[1])


def solution(mesh):
    in_specs = (P(("row", "col"), None), P(("row", "col"), None), P("row", None), P("col", None))
    out_specs = (P("row", None), P("col", None))
    return jax.shard_map(
        per_device, mesh=mesh, in_specs=in_specs, out_specs=out_specs, check_vma=False
    )
```

```python
import functools
import math

import jax
import jax.numpy as jnp
from jax import lax
from jax.experimental import pallas as pl
from jax.experimental.pallas import tpu as pltpu
from jax.sharding import PartitionSpec as P

MESH = pl.DeviceIdType.MESH
F32 = jnp.float32
BF16 = jnp.bfloat16
HIGHEST = lax.Precision.HIGHEST

NZ = 8
NP = 16
SIDE = 4
QUADS = NZ // 2
ZFIRST = 128


def remote(src, dst, ssem, rsem, device):
    return pltpu.make_async_remote_copy(
        src_ref=src, dst_ref=dst, send_sem=ssem, recv_sem=rsem, device_id=device, device_id_type=MESH
    )


def drain(ref, sem):
    pltpu.make_async_copy(ref, ref, sem).wait()


def exchange(
    x_hbm, y_hbm, pi_hbm, pt_hbm,
    img_out, txt_out, gi_out, gt_out,
    X, Y, pi_ref, pt_ref, PT, PI, acc, St,
    JF, JS, JR, JP, RJ, KF, KS, KR, KP, KZ, KZS, KZR, ZS, ZR, FB, G, G2,
    TF, TR, TP, RT, ZT,
    GI, GTS, GTR, XA, YA, YB, XB,
    lsem, ssem, rsem,
):
    z = lax.axis_index("row")
    col = lax.axis_index("col")
    p, c = col // 2, col % 2
    y, x = p // SIDE, p % SIDE
    sib = (z, p * 2 + (1 - c))
    iblock = pi_ref.shape[0]
    half = iblock // 2
    near = half - NP * 16
    lead = ZFIRST
    wide = half - lead
    nt = (((1,), (1,)), ((), ()))

    def chip(k):
        return ((y + k // SIDE) % SIDE) * SIDE + (x + k % SIDE) % SIDE

    def plane_dev(k):
        return (z, chip(k) * 2 + c)

    def z_dev(d):
        return ((z + d) % NZ, col)

    load_t = pltpu.make_async_copy(pt_hbm, pt_ref, lsem.at[2])
    load_i = pltpu.make_async_copy(pi_hbm, pi_ref, lsem.at[3])
    load_t.start()
    load_i.start()
    load_y = pltpu.make_async_copy(y_hbm, Y, lsem.at[0])
    load_x = pltpu.make_async_copy(x_hbm, X, lsem.at[1])
    load_y.start()
    load_x.start()

    barrier = pltpu.get_barrier_semaphore()

    def greet_plane(k, _):
        pl.semaphore_signal(barrier, inc=1, device_id=plane_dev(k), device_id_type=MESH)
        return 0

    def greet_z(d, _):
        pl.semaphore_signal(barrier, inc=1, device_id=z_dev(d), device_id_type=MESH)
        return 0

    lax.fori_loop(1, NZ, greet_z, 0, unroll=True)
    lax.fori_loop(1, NP, greet_plane, 0, unroll=True)
    pl.semaphore_signal(barrier, inc=1, device_id=sib, device_id_type=MESH)
    load_t.wait()
    load_i.wait()
    pl.semaphore_wait(barrier, NZ - 1 + NP - 1 + 1)

    def to_plane(i, src, dst):
        def body(k, _):
            remote(src(k), dst(k), ssem.at[i], rsem.at[i], plane_dev(k)).start()
            return 0

        lax.fori_loop(1, NP, body, 0, unroll=True)

    def to_z(i, src, dst):
        def body(d, _):
            remote(src(d), dst(d), ssem.at[i], rsem.at[i], z_dev(d)).start()
            return 0

        lax.fori_loop(1, NZ, body, 0, unroll=True)

    def to_x(i, buf):
        def body(d, _):
            to = (z, (y * SIDE + (x + d) % SIDE) * 2 + c)
            remote(buf.at[x], buf.at[x], ssem.at[i], rsem.at[i], to).start()
            return 0

        lax.fori_loop(1, SIDE, body, 0, unroll=True)

    def to_y(i, buf):
        def body(d, _):
            to = (z, (((y + d) % SIDE) * SIDE + x) * 2 + c)
            remote(buf.at[y], buf.at[y], ssem.at[i], rsem.at[i], to).start()
            return 0

        lax.fori_loop(1, SIDE, body, 0, unroll=True)

    def total(buf):
        return ((buf[0] + buf[1]) + buf[2]) + buf[3]

    first = pl.ds(pl.multiple_of(c * half, 16), near)
    share = pl.ds(pl.multiple_of(c * half + near + 16 * p, 16), 16)
    slot = pl.ds(pl.multiple_of(near + 16 * p, 16), 16)
    to_z(1, lambda d: pi_ref.at[share], lambda d: PI.at[z, c, slot])

    def to_plane_rows(i, src, dst):
        def body(k, _):
            g = k // SIDE
            remote(src, dst, ssem.at[i + g], rsem.at[i + g], plane_dev(k)).start()
            return 0

        lax.fori_loop(1, NP, body, 0, unroll=True)

    to_plane_rows(28, pt_ref, PT.at[p, c])
    to_z(4, lambda d: pi_ref.at[first], lambda d: PI.at[z, c, pl.ds(0, near)])
    PT[p, c] = pt_ref[...]
    PI[z, c, pl.ds(0, near), :] = pi_ref[first, :]
    PI[z, c, slot, :] = pi_ref[share, :]
    small = PI.at[pl.ds(0, NZ - 1), 0, pl.ds(0, 16)]
    straight = PI.at[pl.ds(0, NZ - 1), 0, pl.ds(0, near)]
    acc[...] = jnp.zeros_like(acc)
    drain(small, rsem.at[1])
    to_plane_rows(32, PI.at[:, c, slot], PI.at[:, c, slot])

    def text_rows(g):
        return pl.ds(((y - g + SIDE) % SIDE) * SIDE, SIDE)

    def image_rows(g):
        return pl.ds(pl.multiple_of(near + 64 * ((y - g + SIDE) % SIDE), 16), 64)

    def hand_text(g):
        drain(PT.at[pl.ds(0, SIDE - 1 if g == 0 else SIDE), 0], rsem.at[28 + g])
        part = PT.at[text_rows(g), c]
        remote(part, part, ssem.at[36 + g], rsem.at[36 + g], sib).start()

    def hand_image(g):
        drain(PI.at[:, 0, pl.ds(0, 48 if g == 0 else 64)], rsem.at[32 + g])
        part = PI.at[:, c, image_rows(g)]
        remote(part, part, ssem.at[40 + g], rsem.at[40 + g], sib).start()

    def text_sketch(g, core):
        row = (y - g + SIDE) % SIDE
        tiles = [
            Y[:, pl.ds(pl.multiple_of(((row * SIDE + j) * 2 + core) * 128, 128), 128)]
            for j in range(SIDE)
        ]
        acc[...] += jnp.dot(
            jnp.concatenate(tiles, axis=1), PT[pl.ds(row * SIDE, SIDE), core].reshape(512, 128),
            preferred_element_type=F32,
        )

    load_y.wait()

    for g in range(SIDE):
        hand_text(g)
        text_sketch(g, c)
    for g in range(SIDE):
        drain(PT.at[pl.ds(0, SIDE), 0], rsem.at[36 + g])
        text_sketch(g, 1 - c)
    St[...] = acc[...].T.astype(BF16)
    load_x.wait()

    def pair(i):
        return (z // 2 + 1 + i) % QUADS

    def image_panel(i, _):
        @pl.when(i < QUADS)
        def _():
            q = pair(i)
            parts = []
            for e in range(2):
                cols = pl.ds(pl.multiple_of((q * 2 + e) * iblock, iblock), iblock)
                parts.append(jnp.dot(St[...], X[:, cols], preferred_element_type=F32))
            for h in range(2):
                both = jnp.concatenate(
                    [d[:, h * half + lead:(h + 1) * half].reshape(NP, 8, wide) for d in parts], axis=1
                )
                JF[h, q] = both
                JS[h, q] = both.astype(BF16)
                for e in range(2):
                    tile = parts[e][:, h * half:h * half + lead]
                    KF[h, q * 2 + e] = tile
                    KS[h, q * 2 + e] = tile.astype(BF16)
            two = pl.ds(q * 2, 2)
            remote(KS.at[1 - c, two], KR.at[two], ssem.at[44 + q], rsem.at[44 + q], sib).start()
            remote(JS.at[1 - c, q], JR.at[q], ssem.at[16 + q], rsem.at[16 + q], sib).start()

        @pl.when(i > 0)
        def _():
            q = pair(i - 1)
            two = pl.ds(q * 2, 2)
            drain(KR.at[two], rsem.at[44 + q])
            KP[two] = (KF[c, two] + KR[two].astype(F32)).astype(BF16)
            for e in range(2):
                to = q * 2 + e

                @pl.when(to != z)
                def _():
                    remote(KP.at[to], KZ.at[z], ssem.at[2], rsem.at[2], (to, col)).start()

            drain(JR.at[q], rsem.at[16 + q])
            JP[q] = (JF[c, q] + JR[q].astype(F32)).astype(BF16)
            to_plane(20 + q, lambda k: JP.at[q, chip(k)], lambda k: RJ.at[q, k - 1])

        return 0

    lax.fori_loop(0, QUADS + 1, image_panel, 0)

    acc[...] = jnp.zeros_like(acc)

    def image_sketch(core, start, width):
        tiles = [
            X[:, pl.ds(pl.multiple_of(e * iblock + core * half + start, 128), width)]
            for e in range(NZ)
        ]
        rows = PI[:, core, pl.ds(start, width)].reshape(NZ * width, 128)
        acc[...] += jnp.dot(
            jnp.concatenate(tiles, axis=1), rows, preferred_element_type=F32
        )

    drain(straight, rsem.at[4])
    part = PI.at[:, c, pl.ds(0, near)]
    remote(part, part, ssem.at[5], rsem.at[5], sib).start()
    image_sketch(c, 0, near)
    for g in range(SIDE):
        hand_image(g)
    image_sketch(c, near, half - near)
    drain(PI.at[:, 0, pl.ds(0, near)], rsem.at[5])
    image_sketch(1 - c, 0, near)
    for g in range(SIDE):
        drain(PI.at[:, 0, pl.ds(0, 64)], rsem.at[40 + g])
    image_sketch(1 - c, near, half - near)
    St[...] = acc[...].T.astype(BF16)

    def quarter(i):
        return (y + 1 + i) % SIDE

    def text_panel(i, _):
        @pl.when(i < SIDE)
        def _():
            r = quarter(i)
            d = jnp.dot(
                St[...], Y[:, pl.ds(pl.multiple_of(r * 1024, 1024), 1024)],
                preferred_element_type=F32,
            )
            for j in range(4):
                for h in range(2):
                    TF[h, r * 4 + j] = d[:, (2 * j + h) * 128:(2 * j + h + 1) * 128]
            rows = pl.ds(r * 4, 4)
            remote(
                TF.at[1 - c, rows], TR.at[rows], ssem.at[24 + r], rsem.at[24 + r], sib
            ).start()

        @pl.when(i > 0)
        def _():
            r = quarter(i - 1)
            rows = pl.ds(r * 4, 4)
            drain(TR.at[rows], rsem.at[24 + r])
            TP[rows] = (TF[c, rows] + TR[rows]).astype(BF16)

            def body(k, _):
                remote(
                    TP.at[chip(k)], RT.at[k - 1], ssem.at[7], rsem.at[7], plane_dev(k)
                ).start()
                return 0

            dy = (r - y + SIDE) % SIDE
            lax.fori_loop(jnp.where(dy == 0, 1, dy * SIDE), dy * SIDE + SIDE, body, 0)

        return 0

    lax.fori_loop(0, SIDE + 1, text_panel, 0)

    def image_sum(i, _):
        q = pair(i)
        drain(RJ.at[q], rsem.at[20 + q])
        own = JF[c, q, p] + JR[q, p].astype(F32)
        own = lax.fori_loop(0, NP - 1, lambda k, a: a + RJ[q, k].astype(F32), own, unroll=True)
        ZS[pl.ds(q * 2, 2)] = own.reshape(2, 8, wide)
        return 0

    lax.fori_loop(0, QUADS, image_sum, 0)
    to_z(8, lambda d: ZS.at[(z + d) % NZ], lambda d: ZR.at[d - 1])

    drain(KZ.at[pl.ds(0, NZ - 1)], rsem.at[2])
    tile = lax.fori_loop(
        1, NZ, lambda d, a: a + KZ[(z + d) % NZ].astype(F32), KF[c, z] + KR[z].astype(F32), unroll=True
    )
    KZS[...] = tile.reshape(NP, 8, lead)
    to_plane(3, lambda k: KZS.at[chip(k)], lambda k: KZR.at[k - 1])

    drain(RT, rsem.at[7])
    town = TF[c, p] + TR[p]
    town = lax.fori_loop(0, NP - 1, lambda k, a: a + RT[k].astype(F32), town, unroll=True)
    ZT[z] = town.astype(BF16)
    to_z(10, lambda d: ZT.at[z], lambda d: ZT.at[z])

    drain(KZR, rsem.at[3])
    FB[:, :lead] = lax.fori_loop(0, NP - 1, lambda k, a: a + KZR[k], KZS[p], unroll=True)
    drain(ZR, rsem.at[8])
    FB[:, lead:] = lax.fori_loop(0, NZ - 1, lambda k, a: a + ZR[k], ZS[z], unroll=True)
    to_plane(9, lambda k: FB, lambda k: G.at[p])
    G[p] = FB[...]

    drain(G.at[pl.ds(0, NP - 1)], rsem.at[9])
    remote(G, G2, ssem.at[11], rsem.at[11], sib).start()
    part = pl.ds(c * 8, 8)

    def gram_rows(ref):
        return lax.dot_general(
            ref[part].reshape(64, half), ref[...].reshape(128, half), nt,
            precision=HIGHEST, preferred_element_type=F32,
        )

    gram = gram_rows(G)
    drain(G2, rsem.at[11])
    GI[z] = gram + gram_rows(G2)
    to_z(12, lambda d: GI.at[z], lambda d: GI.at[z])

    drain(ZT.at[pl.ds(0, NZ - 1)], rsem.at[10])
    block = lax.fori_loop(
        1, NZ, lambda k, a: a + ZT[k].astype(F32), ZT[0].astype(F32), unroll=True
    )
    GTS[...] = lax.dot_general(
        block, block, nt, precision=HIGHEST, preferred_element_type=F32
    ).reshape(2, 64, 128)
    remote(GTS.at[1 - c], GTR, ssem.at[15], rsem.at[15], sib).start()
    txt_out[...] = block.T
    drain(GTR, rsem.at[15])
    own = GTS[c] + GTR[...]
    XA[x] = own[:32]
    YB[y] = own[32:]
    to_x(6, XA)
    to_y(49, YB)

    drain(XA.at[pl.ds(0, SIDE - 1)], rsem.at[6])
    YA[y] = total(XA)
    to_y(48, YA)
    drain(YB.at[pl.ds(0, SIDE - 1)], rsem.at[49])
    XB[x] = total(YB)
    to_x(50, XB)

    lo = pl.ds(pl.multiple_of(c * half, 128), half)
    hi = pl.ds(pl.multiple_of((1 - c) * half, 128), half)
    img_out[lo, :] = G[...].reshape(128, half).T
    img_out[hi, :] = G2[...].reshape(128, half).T

    drain(GI.at[pl.ds(0, NZ - 1)], rsem.at[12])
    mine = pl.ds(pl.multiple_of(c * 64, 64), 64)
    gi_out[mine, :] = lax.fori_loop(1, NZ, lambda k, a: a + GI[k], GI[0], unroll=True)
    remote(gi_out.at[mine], gi_out.at[mine], ssem.at[13], rsem.at[13], sib).start()
    drain(YA.at[pl.ds(0, SIDE - 1)], rsem.at[48])
    gt_out[pl.ds(pl.multiple_of(c * 64, 64), 32), :] = total(YA)
    drain(XB.at[pl.ds(0, SIDE - 1)], rsem.at[50])
    gt_out[pl.ds(pl.multiple_of(c * 64 + 32, 32), 32), :] = total(XB)
    remote(gt_out.at[mine], gt_out.at[mine], ssem.at[14], rsem.at[14], sib).start()
    drain(gi_out.at[pl.ds(0, 64)], rsem.at[13])
    drain(gt_out.at[pl.ds(0, 64)], rsem.at[14])

    drain(small, ssem.at[1])
    drain(KZ.at[pl.ds(0, NZ - 1)], ssem.at[2])
    drain(KZR, ssem.at[3])
    drain(straight, ssem.at[4])
    drain(PI.at[:, 0, pl.ds(0, near)], ssem.at[5])
    drain(PT.at[pl.ds(0, SIDE - 1), 0], ssem.at[28])
    drain(PI.at[:, 0, pl.ds(0, 48)], ssem.at[32])
    drain(XA.at[pl.ds(0, SIDE - 1)], ssem.at[6])
    drain(YA.at[pl.ds(0, SIDE - 1)], ssem.at[48])
    drain(YB.at[pl.ds(0, SIDE - 1)], ssem.at[49])
    drain(XB.at[pl.ds(0, SIDE - 1)], ssem.at[50])
    drain(RT, ssem.at[7])
    drain(ZR, ssem.at[8])
    drain(G.at[pl.ds(0, NP - 1)], ssem.at[9])
    drain(ZT.at[pl.ds(0, NZ - 1)], ssem.at[10])
    drain(G2, ssem.at[11])
    drain(GI.at[pl.ds(0, NZ - 1)], ssem.at[12])
    drain(gi_out.at[pl.ds(0, 64)], ssem.at[13])
    drain(gt_out.at[pl.ds(0, 64)], ssem.at[14])
    drain(GTR, ssem.at[15])

    def left(q, _):
        drain(JR.at[q], ssem.at[16 + q])
        drain(RJ.at[q], ssem.at[20 + q])
        drain(TR.at[pl.ds(q * 4, 4)], ssem.at[24 + q])
        drain(PT.at[pl.ds(0, SIDE), 0], ssem.at[36 + q])
        drain(PI.at[:, 0, pl.ds(0, 64)], ssem.at[40 + q])
        drain(KR.at[pl.ds(q * 2, 2)], ssem.at[44 + q])

        @pl.when(q > 0)
        def _():
            drain(PT.at[pl.ds(0, SIDE), 0], ssem.at[28 + q])
            drain(PI.at[:, 0, pl.ds(0, 64)], ssem.at[32 + q])

        return 0

    lax.fori_loop(0, QUADS, left, 0)


def run_exchange(x, y, pi, pt):
    pairs, dx = x.shape
    dy = y.shape[1]
    rank = 128
    iblock = dx // NZ
    half = iblock // 2
    lead = ZFIRST
    wide = half - lead
    vm = pltpu.VMEM
    scratch = [
        vm((pairs, dx), BF16), vm((pairs, dy), BF16),
        vm((iblock, rank), BF16), vm((128, rank), BF16),
        vm((NP, 2, 128, rank), BF16), vm((NZ, 2, half, rank), BF16),
        vm((pairs, rank), F32), vm((rank, pairs), BF16),
        vm((2, QUADS, NP, 16, wide), F32), vm((2, QUADS, NP, 16, wide), BF16),
        vm((QUADS, NP, 16, wide), BF16), vm((QUADS, NP, 16, wide), BF16),
        vm((QUADS, NP - 1, 16, wide), BF16),
        vm((2, NZ, rank, lead), F32), vm((2, NZ, rank, lead), BF16),
        vm((NZ, rank, lead), BF16), vm((NZ, rank, lead), BF16), vm((NZ, rank, lead), BF16),
        vm((NP, 8, lead), F32), vm((NP - 1, 8, lead), F32),
        vm((NZ, 8, wide), F32), vm((NZ - 1, 8, wide), F32), vm((8, half), F32),
        vm((NP, 8, half), F32), vm((NP, 8, half), F32),
        vm((2, NP, rank, 128), F32), vm((NP, rank, 128), F32),
        vm((NP, rank, 128), BF16), vm((NP - 1, rank, 128), BF16),
        vm((NZ, rank, 128), BF16),
        vm((NZ, 64, 128), F32), vm((2, 64, 128), F32), vm((64, 128), F32),
        vm((SIDE, 32, 128), F32), vm((SIDE, 32, 128), F32), vm((SIDE, 32, 128), F32), vm((SIDE, 32, 128), F32),
        pltpu.SemaphoreType.DMA((4,)), pltpu.SemaphoreType.DMA((51,)), pltpu.SemaphoreType.DMA((51,)),
    ]
    vspec = pl.BlockSpec(memory_space=pltpu.VMEM)
    aspec = pl.BlockSpec(memory_space=pl.ANY)
    square = jax.ShapeDtypeStruct((rank, rank), F32)
    return pl.pallas_call(
        exchange,
        out_shape=(jax.ShapeDtypeStruct((iblock, rank), F32), square, square, square),
        in_specs=[aspec] * 4,
        out_specs=(vspec,) * 4,
        scratch_shapes=scratch,
        name="panels",
        compiler_params=pltpu.CompilerParams(
            collective_id=0, has_side_effects=True, vmem_limit_bytes=60 << 20
        ),
        cost_estimate=pl.CostEstimate(
            flops=4 * pairs * (dx + dy) * rank, bytes_accessed=2 * pairs * (dx + dy), transcendentals=0
        ),
    )(x, y, pi, pt)


def lower_inverses(grams, outer=32):
    n = grams[0].shape[0]
    m = len(grams)
    lane8 = lax.broadcasted_iota(jnp.int32, (8, n), 1)
    sub8 = lax.broadcasted_iota(jnp.int32, (8, n), 0)
    lane = lax.broadcasted_iota(jnp.int32, (n, n), 1)
    laneo = lax.broadcasted_iota(jnp.int32, (outer, n), 1)
    subo = lax.broadcasted_iota(jnp.int32, (outer, n), 0)
    nv = outer // 8
    work = list(grams)
    done = [[] for _ in range(m)]
    for b in range(n // outer):
        j0 = b * outer
        R = [[w[j0 + 8 * v:j0 + 8 * v + 8, :] for v in range(nv)] for w in work]
        rec = [[None] * nv for _ in range(m)]
        scl = [[None] * nv for _ in range(m)]
        for s in range(nv):
            cols = [[[jnp.broadcast_to(R[t][v][:, j0 + 8 * s + k:j0 + 8 * s + k + 1], (8, n)) for v in range(nv)] if True else None
                     for k in range(8)] for t in range(m)]
            for t in range(m):
                rec[t][s] = jnp.zeros((8, n), F32); scl[t][s] = jnp.zeros((8, n), F32)
            for k in range(8):
                j = j0 + 8 * s + k
                for t in range(m):
                    piv = jnp.broadcast_to(cols[t][k][s][k:k + 1, :], (8, n))
                    inv = 1.0 / piv
                    rec[t][s] = jnp.where(sub8 == k, inv, rec[t][s])
                    scl[t][s] = jnp.where(sub8 == k, lax.rsqrt(piv), scl[t][s])
                    prow = jnp.where(lane8 == j, 1.0, jnp.broadcast_to(R[t][s][k:k + 1, :], (8, n)))
                    nxt = {q: jnp.broadcast_to(cols[t][q][s][k:k + 1, :], (8, n)) for q in range(k + 1, 8)}
                    for v in range(s, nv):
                        f = cols[t][k][v] * inv
                        hit = lane8 == j
                        if v == s:
                            f = jnp.where(sub8 > k, f, 0.0)
                            hit = hit & (sub8 >= k)
                            base = jnp.where(hit, jnp.where(sub8 == k, 1.0, 0.0), R[t][v])
                        else:
                            base = jnp.where(hit, 0.0, R[t][v])
                        R[t][v] = base - f * prow
                        for q in range(k + 1, 8):
                            cols[t][q][v] = cols[t][q][v] - f * nxt[q]
        for t in range(m):
            rows = jnp.concatenate(R[t], axis=0)
            inv = jnp.concatenate(rec[t], axis=0)
            scale = jnp.concatenate(scl[t], axis=0)
            done[t].append(jnp.where(laneo <= subo + j0, rows * scale, 0.0))
            if j0 + outer < n:
                right = laneo >= j0 + outer
                fac = jnp.where(right, rows * inv, 0.0)
                keep = jnp.where(right | (laneo <= subo + j0), rows, 0.0)
                upd = lax.dot_general(fac, keep, (((0,), (0,)), ((), ())), precision=HIGHEST, preferred_element_type=F32)
                work[t] = jnp.where((lane >= j0) & (lane < j0 + outer), 0.0, work[t]) - upd
    return [jnp.concatenate(d, axis=0) for d in done]

def finish_kernel(
    img_hbm, txt_hbm, gi_ref, gt_ref, img_out, txt_out, img, txt, sem, *, image_width, text_width
):
    load_i = pltpu.make_async_copy(img_hbm, img, sem.at[0])
    load_t = pltpu.make_async_copy(txt_hbm, txt, sem.at[1])
    load_i.start()
    load_t.start()
    li, lt = lower_inverses([gi_ref[...], gt_ref[...]])
    nt = (((1,), (1,)), ((), ()))
    load_i.wait()
    load_t.wait()
    img_out[...] = lax.dot_general(
        img[...], li * math.sqrt(image_width), nt, precision=HIGHEST, preferred_element_type=F32
    )
    txt_out[...] = lax.dot_general(
        txt[...], lt * math.sqrt(text_width), nt, precision=HIGHEST, preferred_element_type=F32
    )


def finish(img, txt, gi, gt, image_width, text_width):
    vspec = pl.BlockSpec(memory_space=pltpu.VMEM)
    aspec = pl.BlockSpec(memory_space=pl.ANY)
    return pl.pallas_call(
        functools.partial(finish_kernel, image_width=image_width, text_width=text_width),
        out_shape=(jax.ShapeDtypeStruct(img.shape, F32), jax.ShapeDtypeStruct(txt.shape, F32)),
        in_specs=[aspec, aspec, vspec, vspec],
        out_specs=(vspec, vspec),
        scratch_shapes=[
            pltpu.VMEM(img.shape, F32), pltpu.VMEM(txt.shape, F32), pltpu.SemaphoreType.DMA((2,))
        ],
        name="bases",
        compiler_params=pltpu.CompilerParams(vmem_limit_bytes=60 << 20),
    )(img, txt, gi, gt)


def per_device(image_feats, text_feats, probe_image, probe_text):
    img, txt, gi, gt = run_exchange(image_feats, text_feats, probe_image, probe_text)
    return finish(img, txt, gi, gt, image_feats.shape[1], text_feats.shape[1])


def solution(mesh):
    in_specs = (P(("row", "col"), None), P(("row", "col"), None), P("row", None), P("col", None))
    out_specs = (P("row", None), P("col", None))
    return jax.shard_map(
        per_device, mesh=mesh, in_specs=in_specs, out_specs=out_specs, check_vma=False
    )
```

```python
import functools
import math

import jax
import jax.numpy as jnp
from jax import lax
from jax.experimental import pallas as pl
from jax.experimental.pallas import tpu as pltpu
from jax.sharding import PartitionSpec as P

MESH = pl.DeviceIdType.MESH
F32 = jnp.float32
BF16 = jnp.bfloat16
HIGHEST = lax.Precision.HIGHEST

NZ = 8
NP = 16
SIDE = 4
QUADS = NZ // 2
ZFIRST = 128


def remote(src, dst, ssem, rsem, device):
    return pltpu.make_async_remote_copy(
        src_ref=src, dst_ref=dst, send_sem=ssem, recv_sem=rsem, device_id=device, device_id_type=MESH
    )


def drain(ref, sem):
    pltpu.make_async_copy(ref, ref, sem).wait()


def exchange(
    x_hbm, y_hbm, pi_hbm, pt_hbm,
    img_out, txt_out, gi_out, gt_out,
    X, Y, pi_ref, pt_ref, PT, PI, acc, St,
    JF, JS, JR, JP, RJ, KF, KS, KR, KP, KZ, KZS, KZR, ZS, ZR, FB, G, G2,
    TF, TR, TP, RT, ZT,
    GI, TB, GTS, GTR, XA, YA, YB, XB,
    lsem, ssem, rsem,
):
    z = lax.axis_index("row")
    col = lax.axis_index("col")
    p, c = col // 2, col % 2
    y, x = p // SIDE, p % SIDE
    sib = (z, p * 2 + (1 - c))
    iblock = pi_ref.shape[0]
    half = iblock // 2
    near = half - NP * 16
    lead = ZFIRST
    wide = half - lead
    nt = (((1,), (1,)), ((), ()))

    def chip(k):
        return ((y + k // SIDE) % SIDE) * SIDE + (x + k % SIDE) % SIDE

    def plane_dev(k):
        return (z, chip(k) * 2 + c)

    def z_dev(d):
        return ((z + d) % NZ, col)

    load_t = pltpu.make_async_copy(pt_hbm, pt_ref, lsem.at[2])
    load_i = pltpu.make_async_copy(pi_hbm, pi_ref, lsem.at[3])
    load_t.start()
    load_i.start()
    load_y = pltpu.make_async_copy(y_hbm, Y, lsem.at[0])
    load_x = pltpu.make_async_copy(x_hbm, X, lsem.at[1])
    load_y.start()
    load_x.start()

    barrier = pltpu.get_barrier_semaphore()

    def greet_plane(k, _):
        pl.semaphore_signal(barrier, inc=1, device_id=plane_dev(k), device_id_type=MESH)
        return 0

    def greet_z(d, _):
        pl.semaphore_signal(barrier, inc=1, device_id=z_dev(d), device_id_type=MESH)
        return 0

    lax.fori_loop(1, NZ, greet_z, 0, unroll=True)
    lax.fori_loop(1, NP, greet_plane, 0, unroll=True)
    pl.semaphore_signal(barrier, inc=1, device_id=sib, device_id_type=MESH)
    load_t.wait()
    load_i.wait()
    pl.semaphore_wait(barrier, NZ - 1 + NP - 1 + 1)

    def to_plane(i, src, dst):
        def body(k, _):
            remote(src(k), dst(k), ssem.at[i], rsem.at[i], plane_dev(k)).start()
            return 0

        lax.fori_loop(1, NP, body, 0, unroll=True)

    def to_z(i, src, dst):
        def body(d, _):
            remote(src(d), dst(d), ssem.at[i], rsem.at[i], z_dev(d)).start()
            return 0

        lax.fori_loop(1, NZ, body, 0, unroll=True)

    def to_x(i, buf):
        def body(d, _):
            to = (z, (y * SIDE + (x + d) % SIDE) * 2 + c)
            remote(buf.at[x], buf.at[x], ssem.at[i], rsem.at[i], to).start()
            return 0

        lax.fori_loop(1, SIDE, body, 0, unroll=True)

    def to_y(i, buf):
        def body(d, _):
            to = (z, (((y + d) % SIDE) * SIDE + x) * 2 + c)
            remote(buf.at[y], buf.at[y], ssem.at[i], rsem.at[i], to).start()
            return 0

        lax.fori_loop(1, SIDE, body, 0, unroll=True)

    def total(buf):
        return ((buf[0] + buf[1]) + buf[2]) + buf[3]

    first = pl.ds(pl.multiple_of(c * half, 16), near)
    share = pl.ds(pl.multiple_of(c * half + near + 16 * p, 16), 16)
    slot = pl.ds(pl.multiple_of(near + 16 * p, 16), 16)
    to_z(1, lambda d: pi_ref.at[share], lambda d: PI.at[z, c, slot])

    def to_plane_rows(i, src, dst):
        def body(k, _):
            g = k // SIDE
            remote(src, dst, ssem.at[i + g], rsem.at[i + g], plane_dev(k)).start()
            return 0

        lax.fori_loop(1, NP, body, 0, unroll=True)

    to_plane_rows(28, pt_ref, PT.at[p, c])
    to_z(4, lambda d: pi_ref.at[first], lambda d: PI.at[z, c, pl.ds(0, near)])
    PT[p, c] = pt_ref[...]
    PI[z, c, pl.ds(0, near), :] = pi_ref[first, :]
    PI[z, c, slot, :] = pi_ref[share, :]
    small = PI.at[pl.ds(0, NZ - 1), 0, pl.ds(0, 16)]
    straight = PI.at[pl.ds(0, NZ - 1), 0, pl.ds(0, near)]
    acc[...] = jnp.zeros_like(acc)
    drain(small, rsem.at[1])
    to_plane_rows(32, PI.at[:, c, slot], PI.at[:, c, slot])

    def text_rows(g):
        return pl.ds(((y - g + SIDE) % SIDE) * SIDE, SIDE)

    def image_rows(g):
        return pl.ds(pl.multiple_of(near + 64 * ((y - g + SIDE) % SIDE), 16), 64)

    def hand_text(g):
        drain(PT.at[pl.ds(0, SIDE - 1 if g == 0 else SIDE), 0], rsem.at[28 + g])
        part = PT.at[text_rows(g), c]
        remote(part, part, ssem.at[36 + g], rsem.at[36 + g], sib).start()

    def hand_image(g):
        drain(PI.at[:, 0, pl.ds(0, 48 if g == 0 else 64)], rsem.at[32 + g])
        part = PI.at[:, c, image_rows(g)]
        remote(part, part, ssem.at[40 + g], rsem.at[40 + g], sib).start()

    def text_sketch(g, core):
        row = (y - g + SIDE) % SIDE
        tiles = [
            Y[:, pl.ds(pl.multiple_of(((row * SIDE + j) * 2 + core) * 128, 128), 128)]
            for j in range(SIDE)
        ]
        acc[...] += jnp.dot(
            jnp.concatenate(tiles, axis=1), PT[pl.ds(row * SIDE, SIDE), core].reshape(512, 128),
            preferred_element_type=F32,
        )

    load_y.wait()

    for g in range(SIDE):
        hand_text(g)
        text_sketch(g, c)
    for g in range(SIDE):
        drain(PT.at[pl.ds(0, SIDE), 0], rsem.at[36 + g])
        text_sketch(g, 1 - c)
    St[...] = acc[...].T.astype(BF16)
    load_x.wait()

    def pair(i):
        return (z // 2 + 1 + i) % QUADS

    def image_panel(i, _):
        @pl.when(i < QUADS)
        def _():
            q = pair(i)
            parts = []
            for e in range(2):
                cols = pl.ds(pl.multiple_of((q * 2 + e) * iblock, iblock), iblock)
                parts.append(jnp.dot(St[...], X[:, cols], preferred_element_type=F32))
            for h in range(2):
                both = jnp.concatenate(
                    [d[:, h * half + lead:(h + 1) * half].reshape(NP, 8, wide) for d in parts], axis=1
                )
                JF[h, q] = both
                JS[h, q] = both.astype(BF16)
                for e in range(2):
                    tile = parts[e][:, h * half:h * half + lead]
                    KF[h, q * 2 + e] = tile
                    KS[h, q * 2 + e] = tile.astype(BF16)
            two = pl.ds(q * 2, 2)
            remote(KS.at[1 - c, two], KR.at[two], ssem.at[44 + q], rsem.at[44 + q], sib).start()
            remote(JS.at[1 - c, q], JR.at[q], ssem.at[16 + q], rsem.at[16 + q], sib).start()

        @pl.when(i > 0)
        def _():
            q = pair(i - 1)
            two = pl.ds(q * 2, 2)
            drain(KR.at[two], rsem.at[44 + q])
            KP[two] = (KF[c, two] + KR[two].astype(F32)).astype(BF16)
            for e in range(2):
                to = q * 2 + e

                @pl.when(to != z)
                def _():
                    remote(KP.at[to], KZ.at[z], ssem.at[2], rsem.at[2], (to, col)).start()

            drain(JR.at[q], rsem.at[16 + q])
            JP[q] = (JF[c, q] + JR[q].astype(F32)).astype(BF16)
            to_plane(20 + q, lambda k: JP.at[q, chip(k)], lambda k: RJ.at[q, k - 1])

        return 0

    lax.fori_loop(0, QUADS + 1, image_panel, 0)

    acc[...] = jnp.zeros_like(acc)

    def image_sketch(core, start, width):
        tiles = [
            X[:, pl.ds(pl.multiple_of(e * iblock + core * half + start, 128), width)]
            for e in range(NZ)
        ]
        rows = PI[:, core, pl.ds(start, width)].reshape(NZ * width, 128)
        acc[...] += jnp.dot(
            jnp.concatenate(tiles, axis=1), rows, preferred_element_type=F32
        )

    drain(straight, rsem.at[4])
    part = PI.at[:, c, pl.ds(0, near)]
    remote(part, part, ssem.at[5], rsem.at[5], sib).start()
    image_sketch(c, 0, near)
    for g in range(SIDE):
        hand_image(g)
    image_sketch(c, near, half - near)
    drain(PI.at[:, 0, pl.ds(0, near)], rsem.at[5])
    image_sketch(1 - c, 0, near)
    for g in range(SIDE):
        drain(PI.at[:, 0, pl.ds(0, 64)], rsem.at[40 + g])
    image_sketch(1 - c, near, half - near)
    St[...] = acc[...].T.astype(BF16)

    def quarter(i):
        return (y + 1 + i) % SIDE

    def text_panel(i, _):
        @pl.when(i < SIDE)
        def _():
            r = quarter(i)
            d = jnp.dot(
                St[...], Y[:, pl.ds(pl.multiple_of(r * 1024, 1024), 1024)],
                preferred_element_type=F32,
            )
            for j in range(4):
                for h in range(2):
                    TF[h, r * 4 + j] = d[:, (2 * j + h) * 128:(2 * j + h + 1) * 128]
            rows = pl.ds(r * 4, 4)
            remote(
                TF.at[1 - c, rows], TR.at[rows], ssem.at[24 + r], rsem.at[24 + r], sib
            ).start()

        @pl.when(i > 0)
        def _():
            r = quarter(i - 1)
            rows = pl.ds(r * 4, 4)
            drain(TR.at[rows], rsem.at[24 + r])
            TP[rows] = (TF[c, rows] + TR[rows]).astype(BF16)

            def body(k, _):
                remote(
                    TP.at[chip(k)], RT.at[k - 1], ssem.at[7], rsem.at[7], plane_dev(k)
                ).start()
                return 0

            dy = (r - y + SIDE) % SIDE
            lax.fori_loop(jnp.where(dy == 0, 1, dy * SIDE), dy * SIDE + SIDE, body, 0)

        return 0

    lax.fori_loop(0, SIDE + 1, text_panel, 0)

    def image_sum(i, _):
        q = pair(i)
        drain(RJ.at[q], rsem.at[20 + q])
        own = JF[c, q, p] + JR[q, p].astype(F32)
        own = lax.fori_loop(0, NP - 1, lambda k, a: a + RJ[q, k].astype(F32), own, unroll=True)
        ZS[pl.ds(q * 2, 2)] = own.reshape(2, 8, wide)
        return 0

    lax.fori_loop(0, QUADS, image_sum, 0)
    to_z(8, lambda d: ZS.at[(z + d) % NZ], lambda d: ZR.at[d - 1])

    drain(KZ.at[pl.ds(0, NZ - 1)], rsem.at[2])
    tile = lax.fori_loop(
        1, NZ, lambda d, a: a + KZ[(z + d) % NZ].astype(F32), KF[c, z] + KR[z].astype(F32), unroll=True
    )
    KZS[...] = tile.reshape(NP, 8, lead)
    to_plane(3, lambda k: KZS.at[chip(k)], lambda k: KZR.at[k - 1])

    drain(RT, rsem.at[7])
    town = TF[c, p] + TR[p]
    town = lax.fori_loop(0, NP - 1, lambda k, a: a + RT[k].astype(F32), town, unroll=True)
    ZT[z] = town.astype(BF16)
    to_z(10, lambda d: ZT.at[z], lambda d: ZT.at[z])

    drain(KZR, rsem.at[3])
    FB[:, :lead] = lax.fori_loop(0, NP - 1, lambda k, a: a + KZR[k], KZS[p], unroll=True)
    drain(ZR, rsem.at[8])
    FB[:, lead:] = lax.fori_loop(0, NZ - 1, lambda k, a: a + ZR[k], ZS[z], unroll=True)
    to_plane(9, lambda k: FB, lambda k: G.at[p])
    G[p] = FB[...]

    drain(G.at[pl.ds(0, NP - 1)], rsem.at[9])
    remote(G, G2, ssem.at[11], rsem.at[11], sib).start()
    part = pl.ds(c * 8, 8)

    def gram_rows(ref):
        return lax.dot_general(
            ref[part].reshape(64, half), ref[...].reshape(128, half), nt,
            precision=HIGHEST, preferred_element_type=F32,
        )

    gram = gram_rows(G)
    drain(G2, rsem.at[11])
    GI[z] = gram + gram_rows(G2)
    to_z(12, lambda d: GI.at[z], lambda d: GI.at[z])

    drain(ZT.at[pl.ds(0, NZ - 1)], rsem.at[10])
    block = lax.fori_loop(
        1, NZ, lambda k, a: a + ZT[k].astype(F32), ZT[0].astype(F32), unroll=True
    )
    TB[...] = block

    def text_rows_gram(h):
        rows = TB[pl.ds(pl.multiple_of(h * 64, 64), 64), :]
        GTS[h] = lax.dot_general(
            rows, TB[...], nt, precision=HIGHEST, preferred_element_type=F32
        )

    text_rows_gram(1 - c)
    remote(GTS.at[1 - c], GTR, ssem.at[15], rsem.at[15], sib).start()
    text_rows_gram(c)
    txt_out[...] = block.T
    drain(GTR, rsem.at[15])
    own = GTS[c] + GTR[...]
    XA[x] = own[:32]
    YB[y] = own[32:]
    to_x(6, XA)
    to_y(49, YB)

    drain(XA.at[pl.ds(0, SIDE - 1)], rsem.at[6])
    YA[y] = total(XA)
    to_y(48, YA)
    drain(YB.at[pl.ds(0, SIDE - 1)], rsem.at[49])
    XB[x] = total(YB)
    to_x(50, XB)

    lo = pl.ds(pl.multiple_of(c * half, 128), half)
    hi = pl.ds(pl.multiple_of((1 - c) * half, 128), half)
    img_out[lo, :] = G[...].reshape(128, half).T
    img_out[hi, :] = G2[...].reshape(128, half).T

    drain(small, ssem.at[1])
    drain(KZ.at[pl.ds(0, NZ - 1)], ssem.at[2])
    drain(KZR, ssem.at[3])
    drain(straight, ssem.at[4])
    drain(PI.at[:, 0, pl.ds(0, near)], ssem.at[5])
    drain(PT.at[pl.ds(0, SIDE - 1), 0], ssem.at[28])
    drain(PI.at[:, 0, pl.ds(0, 48)], ssem.at[32])
    drain(RT, ssem.at[7])
    drain(ZR, ssem.at[8])
    drain(G.at[pl.ds(0, NP - 1)], ssem.at[9])
    drain(ZT.at[pl.ds(0, NZ - 1)], ssem.at[10])
    drain(G2, ssem.at[11])

    def left(q, _):
        drain(JR.at[q], ssem.at[16 + q])
        drain(RJ.at[q], ssem.at[20 + q])
        drain(TR.at[pl.ds(q * 4, 4)], ssem.at[24 + q])
        drain(PT.at[pl.ds(0, SIDE), 0], ssem.at[36 + q])
        drain(PI.at[:, 0, pl.ds(0, 64)], ssem.at[40 + q])
        drain(KR.at[pl.ds(q * 2, 2)], ssem.at[44 + q])

        @pl.when(q > 0)
        def _():
            drain(PT.at[pl.ds(0, SIDE), 0], ssem.at[28 + q])
            drain(PI.at[:, 0, pl.ds(0, 64)], ssem.at[32 + q])

        return 0

    lax.fori_loop(0, QUADS, left, 0)

    drain(GI.at[pl.ds(0, NZ - 1)], rsem.at[12])
    mine = pl.ds(pl.multiple_of(c * 64, 64), 64)
    gi_out[mine, :] = lax.fori_loop(1, NZ, lambda k, a: a + GI[k], GI[0], unroll=True)
    remote(gi_out.at[mine], gi_out.at[mine], ssem.at[13], rsem.at[13], sib).start()
    drain(YA.at[pl.ds(0, SIDE - 1)], rsem.at[48])
    gt_out[pl.ds(pl.multiple_of(c * 64, 64), 32), :] = total(YA)
    drain(XB.at[pl.ds(0, SIDE - 1)], rsem.at[50])
    gt_out[pl.ds(pl.multiple_of(c * 64 + 32, 32), 32), :] = total(XB)
    remote(gt_out.at[mine], gt_out.at[mine], ssem.at[14], rsem.at[14], sib).start()
    drain(gi_out.at[pl.ds(0, 64)], rsem.at[13])
    drain(gt_out.at[pl.ds(0, 64)], rsem.at[14])

    drain(XA.at[pl.ds(0, SIDE - 1)], ssem.at[6])
    drain(YA.at[pl.ds(0, SIDE - 1)], ssem.at[48])
    drain(YB.at[pl.ds(0, SIDE - 1)], ssem.at[49])
    drain(XB.at[pl.ds(0, SIDE - 1)], ssem.at[50])
    drain(GI.at[pl.ds(0, NZ - 1)], ssem.at[12])
    drain(gi_out.at[pl.ds(0, 64)], ssem.at[13])
    drain(gt_out.at[pl.ds(0, 64)], ssem.at[14])
    drain(GTR, ssem.at[15])


def run_exchange(x, y, pi, pt):
    pairs, dx = x.shape
    dy = y.shape[1]
    rank = 128
    iblock = dx // NZ
    half = iblock // 2
    lead = ZFIRST
    wide = half - lead
    vm = pltpu.VMEM
    scratch = [
        vm((pairs, dx), BF16), vm((pairs, dy), BF16),
        vm((iblock, rank), BF16), vm((128, rank), BF16),
        vm((NP, 2, 128, rank), BF16), vm((NZ, 2, half, rank), BF16),
        vm((pairs, rank), F32), vm((rank, pairs), BF16),
        vm((2, QUADS, NP, 16, wide), F32), vm((2, QUADS, NP, 16, wide), BF16),
        vm((QUADS, NP, 16, wide), BF16), vm((QUADS, NP, 16, wide), BF16),
        vm((QUADS, NP - 1, 16, wide), BF16),
        vm((2, NZ, rank, lead), F32), vm((2, NZ, rank, lead), BF16),
        vm((NZ, rank, lead), BF16), vm((NZ, rank, lead), BF16), vm((NZ, rank, lead), BF16),
        vm((NP, 8, lead), F32), vm((NP - 1, 8, lead), F32),
        vm((NZ, 8, wide), F32), vm((NZ - 1, 8, wide), F32), vm((8, half), F32),
        vm((NP, 8, half), F32), vm((NP, 8, half), F32),
        vm((2, NP, rank, 128), F32), vm((NP, rank, 128), F32),
        vm((NP, rank, 128), BF16), vm((NP - 1, rank, 128), BF16),
        vm((NZ, rank, 128), BF16),
        vm((NZ, 64, 128), F32), vm((rank, 128), F32), vm((2, 64, 128), F32), vm((64, 128), F32),
        vm((SIDE, 32, 128), F32), vm((SIDE, 32, 128), F32), vm((SIDE, 32, 128), F32), vm((SIDE, 32, 128), F32),
        pltpu.SemaphoreType.DMA((4,)), pltpu.SemaphoreType.DMA((51,)), pltpu.SemaphoreType.DMA((51,)),
    ]
    vspec = pl.BlockSpec(memory_space=pltpu.VMEM)
    aspec = pl.BlockSpec(memory_space=pl.ANY)
    square = jax.ShapeDtypeStruct((rank, rank), F32)
    return pl.pallas_call(
        exchange,
        out_shape=(jax.ShapeDtypeStruct((iblock, rank), F32), square, square, square),
        in_specs=[aspec] * 4,
        out_specs=(vspec,) * 4,
        scratch_shapes=scratch,
        name="panels",
        compiler_params=pltpu.CompilerParams(
            collective_id=0, has_side_effects=True, vmem_limit_bytes=60 << 20
        ),
        cost_estimate=pl.CostEstimate(
            flops=4 * pairs * (dx + dy) * rank, bytes_accessed=2 * pairs * (dx + dy), transcendentals=0
        ),
    )(x, y, pi, pt)


def lower_inverses(grams, outer=32):
    n = grams[0].shape[0]
    m = len(grams)
    lane8 = lax.broadcasted_iota(jnp.int32, (8, n), 1)
    sub8 = lax.broadcasted_iota(jnp.int32, (8, n), 0)
    lane = lax.broadcasted_iota(jnp.int32, (n, n), 1)
    laneo = lax.broadcasted_iota(jnp.int32, (outer, n), 1)
    subo = lax.broadcasted_iota(jnp.int32, (outer, n), 0)
    nv = outer // 8
    work = list(grams)
    done = [[] for _ in range(m)]
    for b in range(n // outer):
        j0 = b * outer
        R = [[w[j0 + 8 * v:j0 + 8 * v + 8, :] for v in range(nv)] for w in work]
        rec = [[None] * nv for _ in range(m)]
        scl = [[None] * nv for _ in range(m)]
        for s in range(nv):
            cols = [[[jnp.broadcast_to(R[t][v][:, j0 + 8 * s + k:j0 + 8 * s + k + 1], (8, n)) for v in range(nv)] if True else None
                     for k in range(8)] for t in range(m)]
            for t in range(m):
                rec[t][s] = jnp.zeros((8, n), F32); scl[t][s] = jnp.zeros((8, n), F32)
            for k in range(8):
                j = j0 + 8 * s + k
                for t in range(m):
                    piv = jnp.broadcast_to(cols[t][k][s][k:k + 1, :], (8, n))
                    inv = 1.0 / piv
                    rec[t][s] = jnp.where(sub8 == k, inv, rec[t][s])
                    scl[t][s] = jnp.where(sub8 == k, lax.rsqrt(piv), scl[t][s])
                    prow = jnp.where(lane8 == j, 1.0, jnp.broadcast_to(R[t][s][k:k + 1, :], (8, n)))
                    nxt = {q: jnp.broadcast_to(cols[t][q][s][k:k + 1, :], (8, n)) for q in range(k + 1, 8)}
                    for v in range(s, nv):
                        f = cols[t][k][v] * inv
                        hit = lane8 == j
                        if v == s:
                            f = jnp.where(sub8 > k, f, 0.0)
                            hit = hit & (sub8 >= k)
                            base = jnp.where(hit, jnp.where(sub8 == k, 1.0, 0.0), R[t][v])
                        else:
                            base = jnp.where(hit, 0.0, R[t][v])
                        R[t][v] = base - f * prow
                        for q in range(k + 1, 8):
                            cols[t][q][v] = cols[t][q][v] - f * nxt[q]
        for t in range(m):
            rows = jnp.concatenate(R[t], axis=0)
            inv = jnp.concatenate(rec[t], axis=0)
            scale = jnp.concatenate(scl[t], axis=0)
            done[t].append(jnp.where(laneo <= subo + j0, rows * scale, 0.0))
            if j0 + outer < n:
                right = laneo >= j0 + outer
                fac = jnp.where(right, rows * inv, 0.0)
                keep = jnp.where(right | (laneo <= subo + j0), rows, 0.0)
                upd = lax.dot_general(fac, keep, (((0,), (0,)), ((), ())), precision=HIGHEST, preferred_element_type=F32)
                work[t] = jnp.where((lane >= j0) & (lane < j0 + outer), 0.0, work[t]) - upd
    return [jnp.concatenate(d, axis=0) for d in done]

def product_nt(a, b):
    def split(v):
        high = v.astype(BF16)
        return high, (v - high.astype(F32)).astype(BF16)

    def dot(u, v):
        return lax.dot_general(u, v, (((1,), (1,)), ((), ())), preferred_element_type=F32)

    (ah, al), (bh, bl) = split(a), split(b)
    return dot(ah, bh) + (dot(ah, bl) + dot(al, bh))


def finish_kernel(
    img_hbm, txt_hbm, gi_ref, gt_ref, img_out, txt_out, img, txt, sem, *, image_width, text_width
):
    load_i = pltpu.make_async_copy(img_hbm, img, sem.at[0])
    load_t = pltpu.make_async_copy(txt_hbm, txt, sem.at[1])
    load_i.start()
    load_t.start()
    li, lt = lower_inverses([gi_ref[...], gt_ref[...]])
    load_i.wait()
    load_t.wait()
    img_out[...] = product_nt(img[...], li * math.sqrt(image_width))
    txt_out[...] = product_nt(txt[...], lt * math.sqrt(text_width))


def finish(img, txt, gi, gt, image_width, text_width):
    vspec = pl.BlockSpec(memory_space=pltpu.VMEM)
    aspec = pl.BlockSpec(memory_space=pl.ANY)
    return pl.pallas_call(
        functools.partial(finish_kernel, image_width=image_width, text_width=text_width),
        out_shape=(jax.ShapeDtypeStruct(img.shape, F32), jax.ShapeDtypeStruct(txt.shape, F32)),
        in_specs=[aspec, aspec, vspec, vspec],
        out_specs=(vspec, vspec),
        scratch_shapes=[
            pltpu.VMEM(img.shape, F32), pltpu.VMEM(txt.shape, F32), pltpu.SemaphoreType.DMA((2,))
        ],
        name="bases",
        compiler_params=pltpu.CompilerParams(vmem_limit_bytes=60 << 20),
    )(img, txt, gi, gt)


def per_device(image_feats, text_feats, probe_image, probe_text):
    img, txt, gi, gt = run_exchange(image_feats, text_feats, probe_image, probe_text)
    return finish(img, txt, gi, gt, image_feats.shape[1], text_feats.shape[1])


def solution(mesh):
    in_specs = (P(("row", "col"), None), P(("row", "col"), None), P("row", None), P("col", None))
    out_specs = (P("row", None), P("col", None))
    return jax.shard_map(
        per_device, mesh=mesh, in_specs=in_specs, out_specs=out_specs, check_vma=False
    )
```

```python
import functools
import math

import jax
import jax.numpy as jnp
from jax import lax
from jax.experimental import pallas as pl
from jax.experimental.pallas import tpu as pltpu
from jax.sharding import PartitionSpec as P

MESH = pl.DeviceIdType.MESH
F32 = jnp.float32
BF16 = jnp.bfloat16
HIGHEST = lax.Precision.HIGHEST

NZ = 8
NP = 16
SIDE = 4
QUADS = NZ // 2
ZFIRST = 128


def remote(src, dst, ssem, rsem, device):
    return pltpu.make_async_remote_copy(
        src_ref=src, dst_ref=dst, send_sem=ssem, recv_sem=rsem, device_id=device, device_id_type=MESH
    )


def drain(ref, sem):
    pltpu.make_async_copy(ref, ref, sem).wait()


def exchange(
    x_hbm, y_hbm, pi_hbm, pt_hbm,
    img_out, txt_out, gi_out, gt_out,
    X, Y, pi_ref, pt_ref, PT, PI, acc, St,
    JF, JS, JR, JP, RJ, KF, KS, KR, KP, KZ, KZS, KZR, ZS, ZR, FB, G, G2,
    TF, TR, TP, RT, ZT,
    GI, TB, GTS, GTR, XA, YA, YB, XB,
    lsem, ssem, rsem,
):
    z = lax.axis_index("row")
    col = lax.axis_index("col")
    p, c = col // 2, col % 2
    y, x = p // SIDE, p % SIDE
    sib = (z, p * 2 + (1 - c))
    iblock = pi_ref.shape[0]
    half = iblock // 2
    near = half - NP * 16
    lead = ZFIRST
    wide = half - lead
    nt = (((1,), (1,)), ((), ()))

    def chip(k):
        return ((y + k // SIDE) % SIDE) * SIDE + (x + k % SIDE) % SIDE

    def plane_dev(k):
        return (z, chip(k) * 2 + c)

    def z_dev(d):
        return ((z + d) % NZ, col)

    load_t = pltpu.make_async_copy(pt_hbm, pt_ref, lsem.at[2])
    load_i = pltpu.make_async_copy(pi_hbm, pi_ref, lsem.at[3])
    load_t.start()
    load_i.start()
    load_y = pltpu.make_async_copy(y_hbm, Y, lsem.at[0])
    load_x = pltpu.make_async_copy(x_hbm, X, lsem.at[1])
    load_y.start()
    load_x.start()

    barrier = pltpu.get_barrier_semaphore()

    def greet_plane(k, _):
        pl.semaphore_signal(barrier, inc=1, device_id=plane_dev(k), device_id_type=MESH)
        return 0

    def greet_z(d, _):
        pl.semaphore_signal(barrier, inc=1, device_id=z_dev(d), device_id_type=MESH)
        return 0

    lax.fori_loop(1, NZ, greet_z, 0, unroll=True)
    lax.fori_loop(1, NP, greet_plane, 0, unroll=True)
    pl.semaphore_signal(barrier, inc=1, device_id=sib, device_id_type=MESH)
    load_t.wait()
    load_i.wait()
    pl.semaphore_wait(barrier, NZ - 1 + NP - 1 + 1)

    def to_plane(i, src, dst):
        def body(k, _):
            remote(src(k), dst(k), ssem.at[i], rsem.at[i], plane_dev(k)).start()
            return 0

        lax.fori_loop(1, NP, body, 0, unroll=True)

    def to_z(i, src, dst):
        def body(d, _):
            remote(src(d), dst(d), ssem.at[i], rsem.at[i], z_dev(d)).start()
            return 0

        lax.fori_loop(1, NZ, body, 0, unroll=True)

    def to_x(i, buf):
        def body(d, _):
            to = (z, (y * SIDE + (x + d) % SIDE) * 2 + c)
            remote(buf.at[x], buf.at[x], ssem.at[i], rsem.at[i], to).start()
            return 0

        lax.fori_loop(1, SIDE, body, 0, unroll=True)

    def to_y(i, buf):
        def body(d, _):
            to = (z, (((y + d) % SIDE) * SIDE + x) * 2 + c)
            remote(buf.at[y], buf.at[y], ssem.at[i], rsem.at[i], to).start()
            return 0

        lax.fori_loop(1, SIDE, body, 0, unroll=True)

    def total(buf):
        return ((buf[0] + buf[1]) + buf[2]) + buf[3]

    first = pl.ds(pl.multiple_of(c * half, 16), near)
    share = pl.ds(pl.multiple_of(c * half + near + 16 * p, 16), 16)
    slot = pl.ds(pl.multiple_of(near + 16 * p, 16), 16)

    def to_plane_rows(i, src, dst):
        def body(k, _):
            g = k // SIDE
            remote(src, dst, ssem.at[i + g], rsem.at[i + g], plane_dev(k)).start()
            return 0

        lax.fori_loop(1, NP, body, 0, unroll=True)

    to_plane_rows(28, pt_ref, PT.at[p, c])
    to_z(1, lambda d: pi_ref.at[share], lambda d: PI.at[z, c, slot])
    to_z(4, lambda d: pi_ref.at[first], lambda d: PI.at[z, c, pl.ds(0, near)])
    PT[p, c] = pt_ref[...]
    PI[z, c, pl.ds(0, near), :] = pi_ref[first, :]
    PI[z, c, slot, :] = pi_ref[share, :]
    small = PI.at[pl.ds(0, NZ - 1), 0, pl.ds(0, 16)]
    straight = PI.at[pl.ds(0, NZ - 1), 0, pl.ds(0, near)]
    acc[...] = jnp.zeros_like(acc)
    drain(small, rsem.at[1])
    to_plane_rows(32, PI.at[:, c, slot], PI.at[:, c, slot])

    def text_rows(g):
        return pl.ds(((y - g + SIDE) % SIDE) * SIDE, SIDE)

    def image_rows(g):
        return pl.ds(pl.multiple_of(near + 64 * ((y - g + SIDE) % SIDE), 16), 64)

    def hand_text(g):
        drain(PT.at[pl.ds(0, SIDE - 1 if g == 0 else SIDE), 0], rsem.at[28 + g])
        part = PT.at[text_rows(g), c]
        remote(part, part, ssem.at[36 + g], rsem.at[36 + g], sib).start()

    def hand_image(g):
        drain(PI.at[:, 0, pl.ds(0, 48 if g == 0 else 64)], rsem.at[32 + g])
        part = PI.at[:, c, image_rows(g)]
        remote(part, part, ssem.at[40 + g], rsem.at[40 + g], sib).start()

    def text_sketch(g, core):
        row = (y - g + SIDE) % SIDE
        tiles = [
            Y[:, pl.ds(pl.multiple_of(((row * SIDE + j) * 2 + core) * 128, 128), 128)]
            for j in range(SIDE)
        ]
        acc[...] += jnp.dot(
            jnp.concatenate(tiles, axis=1), PT[pl.ds(row * SIDE, SIDE), core].reshape(512, 128),
            preferred_element_type=F32,
        )

    load_y.wait()

    for g in range(SIDE):
        hand_text(g)
        text_sketch(g, c)
    for g in range(SIDE):
        drain(PT.at[pl.ds(0, SIDE), 0], rsem.at[36 + g])
        text_sketch(g, 1 - c)
    St[...] = acc[...].T.astype(BF16)
    load_x.wait()

    def pair(i):
        return (z // 2 + 1 + i) % QUADS

    def image_panel(i, _):
        @pl.when(i < QUADS)
        def _():
            q = pair(i)
            parts = []
            for e in range(2):
                cols = pl.ds(pl.multiple_of((q * 2 + e) * iblock, iblock), iblock)
                parts.append(jnp.dot(St[...], X[:, cols], preferred_element_type=F32))
            for h in range(2):
                both = jnp.concatenate(
                    [d[:, h * half + lead:(h + 1) * half].reshape(NP, 8, wide) for d in parts], axis=1
                )
                JF[h, q] = both
                JS[h, q] = both.astype(BF16)
                for e in range(2):
                    tile = parts[e][:, h * half:h * half + lead]
                    KF[h, q * 2 + e] = tile
                    KS[h, q * 2 + e] = tile.astype(BF16)
            two = pl.ds(q * 2, 2)
            remote(KS.at[1 - c, two], KR.at[two], ssem.at[44 + q], rsem.at[44 + q], sib).start()
            remote(JS.at[1 - c, q], JR.at[q], ssem.at[16 + q], rsem.at[16 + q], sib).start()

        @pl.when(i > 0)
        def _():
            q = pair(i - 1)
            two = pl.ds(q * 2, 2)
            drain(KR.at[two], rsem.at[44 + q])
            KP[two] = (KF[c, two] + KR[two].astype(F32)).astype(BF16)
            for e in range(2):
                to = q * 2 + e

                @pl.when(to != z)
                def _():
                    remote(KP.at[to], KZ.at[z], ssem.at[2], rsem.at[2], (to, col)).start()

            drain(JR.at[q], rsem.at[16 + q])
            JP[q] = (JF[c, q] + JR[q].astype(F32)).astype(BF16)
            to_plane(20 + q, lambda k: JP.at[q, chip(k)], lambda k: RJ.at[q, k - 1])

        return 0

    lax.fori_loop(0, QUADS + 1, image_panel, 0)

    acc[...] = jnp.zeros_like(acc)

    def image_sketch(core, start, width):
        tiles = [
            X[:, pl.ds(pl.multiple_of(e * iblock + core * half + start, 128), width)]
            for e in range(NZ)
        ]
        rows = PI[:, core, pl.ds(start, width)].reshape(NZ * width, 128)
        acc[...] += jnp.dot(
            jnp.concatenate(tiles, axis=1), rows, preferred_element_type=F32
        )

    drain(straight, rsem.at[4])
    part = PI.at[:, c, pl.ds(0, near)]
    remote(part, part, ssem.at[5], rsem.at[5], sib).start()
    image_sketch(c, 0, near)
    for g in range(SIDE):
        hand_image(g)
    image_sketch(c, near, half - near)
    drain(PI.at[:, 0, pl.ds(0, near)], rsem.at[5])
    image_sketch(1 - c, 0, near)
    for g in range(SIDE):
        drain(PI.at[:, 0, pl.ds(0, 64)], rsem.at[40 + g])
    image_sketch(1 - c, near, half - near)
    St[...] = acc[...].T.astype(BF16)

    def quarter(i):
        return (y + 1 + i) % SIDE

    def text_panel(i, _):
        @pl.when(i < SIDE)
        def _():
            r = quarter(i)
            d = jnp.dot(
                St[...], Y[:, pl.ds(pl.multiple_of(r * 1024, 1024), 1024)],
                preferred_element_type=F32,
            )
            for j in range(4):
                for h in range(2):
                    TF[h, r * 4 + j] = d[:, (2 * j + h) * 128:(2 * j + h + 1) * 128]
            rows = pl.ds(r * 4, 4)
            remote(
                TF.at[1 - c, rows], TR.at[rows], ssem.at[24 + r], rsem.at[24 + r], sib
            ).start()

        @pl.when(i > 0)
        def _():
            r = quarter(i - 1)
            rows = pl.ds(r * 4, 4)
            drain(TR.at[rows], rsem.at[24 + r])
            TP[rows] = (TF[c, rows] + TR[rows]).astype(BF16)

            def body(k, _):
                remote(
                    TP.at[chip(k)], RT.at[k - 1], ssem.at[7], rsem.at[7], plane_dev(k)
                ).start()
                return 0

            dy = (r - y + SIDE) % SIDE
            lax.fori_loop(jnp.where(dy == 0, 1, dy * SIDE), dy * SIDE + SIDE, body, 0)

        return 0

    lax.fori_loop(0, SIDE + 1, text_panel, 0)

    def image_sum(i, _):
        q = pair(i)
        drain(RJ.at[q], rsem.at[20 + q])
        own = JF[c, q, p] + JR[q, p].astype(F32)
        own = lax.fori_loop(0, NP - 1, lambda k, a: a + RJ[q, k].astype(F32), own, unroll=True)
        ZS[pl.ds(q * 2, 2)] = own.reshape(2, 8, wide)
        return 0

    lax.fori_loop(0, QUADS, image_sum, 0)
    to_z(8, lambda d: ZS.at[(z + d) % NZ], lambda d: ZR.at[d - 1])

    drain(KZ.at[pl.ds(0, NZ - 1)], rsem.at[2])
    tile = lax.fori_loop(
        1, NZ, lambda d, a: a + KZ[(z + d) % NZ].astype(F32), KF[c, z] + KR[z].astype(F32), unroll=True
    )
    KZS[...] = tile.reshape(NP, 8, lead)
    to_plane(3, lambda k: KZS.at[chip(k)], lambda k: KZR.at[k - 1])

    drain(RT, rsem.at[7])
    town = TF[c, p] + TR[p]
    town = lax.fori_loop(0, NP - 1, lambda k, a: a + RT[k].astype(F32), town, unroll=True)
    ZT[z] = town.astype(BF16)
    to_z(10, lambda d: ZT.at[z], lambda d: ZT.at[z])

    drain(KZR, rsem.at[3])
    FB[:, :lead] = lax.fori_loop(0, NP - 1, lambda k, a: a + KZR[k], KZS[p], unroll=True)
    drain(ZR, rsem.at[8])
    FB[:, lead:] = lax.fori_loop(0, NZ - 1, lambda k, a: a + ZR[k], ZS[z], unroll=True)
    to_plane(9, lambda k: FB, lambda k: G.at[p])
    G[p] = FB[...]

    drain(G.at[pl.ds(0, NP - 1)], rsem.at[9])
    remote(G, G2, ssem.at[11], rsem.at[11], sib).start()
    part = pl.ds(c * 8, 8)

    def gram_rows(ref):
        return lax.dot_general(
            ref[part].reshape(64, half), ref[...].reshape(128, half), nt,
            precision=HIGHEST, preferred_element_type=F32,
        )

    gram = gram_rows(G)
    drain(G2, rsem.at[11])
    GI[z] = gram + gram_rows(G2)
    to_z(12, lambda d: GI.at[z], lambda d: GI.at[z])

    drain(ZT.at[pl.ds(0, NZ - 1)], rsem.at[10])
    block = lax.fori_loop(
        1, NZ, lambda k, a: a + ZT[k].astype(F32), ZT[0].astype(F32), unroll=True
    )
    TB[...] = block

    def text_rows_gram(h):
        rows = TB[pl.ds(pl.multiple_of(h * 64, 64), 64), :]
        GTS[h] = lax.dot_general(
            rows, TB[...], nt, precision=HIGHEST, preferred_element_type=F32
        )

    text_rows_gram(1 - c)
    remote(GTS.at[1 - c], GTR, ssem.at[15], rsem.at[15], sib).start()
    text_rows_gram(c)
    txt_out[...] = block.T
    drain(GTR, rsem.at[15])
    own = GTS[c] + GTR[...]
    XA[x] = own[:32]
    YB[y] = own[32:]
    to_x(6, XA)
    to_y(49, YB)

    drain(XA.at[pl.ds(0, SIDE - 1)], rsem.at[6])
    YA[y] = total(XA)
    to_y(48, YA)
    drain(YB.at[pl.ds(0, SIDE - 1)], rsem.at[49])
    XB[x] = total(YB)
    to_x(50, XB)

    lo = pl.ds(pl.multiple_of(c * half, 128), half)
    hi = pl.ds(pl.multiple_of((1 - c) * half, 128), half)
    img_out[lo, :] = G[...].reshape(128, half).T
    img_out[hi, :] = G2[...].reshape(128, half).T

    drain(small, ssem.at[1])
    drain(KZ.at[pl.ds(0, NZ - 1)], ssem.at[2])
    drain(KZR, ssem.at[3])
    drain(straight, ssem.at[4])
    drain(PI.at[:, 0, pl.ds(0, near)], ssem.at[5])
    drain(PT.at[pl.ds(0, SIDE - 1), 0], ssem.at[28])
    drain(PI.at[:, 0, pl.ds(0, 48)], ssem.at[32])
    drain(RT, ssem.at[7])
    drain(ZR, ssem.at[8])
    drain(G.at[pl.ds(0, NP - 1)], ssem.at[9])
    drain(ZT.at[pl.ds(0, NZ - 1)], ssem.at[10])
    drain(G2, ssem.at[11])

    def left(q, _):
        drain(JR.at[q], ssem.at[16 + q])
        drain(RJ.at[q], ssem.at[20 + q])
        drain(TR.at[pl.ds(q * 4, 4)], ssem.at[24 + q])
        drain(PT.at[pl.ds(0, SIDE), 0], ssem.at[36 + q])
        drain(PI.at[:, 0, pl.ds(0, 64)], ssem.at[40 + q])
        drain(KR.at[pl.ds(q * 2, 2)], ssem.at[44 + q])

        @pl.when(q > 0)
        def _():
            drain(PT.at[pl.ds(0, SIDE), 0], ssem.at[28 + q])
            drain(PI.at[:, 0, pl.ds(0, 64)], ssem.at[32 + q])

        return 0

    lax.fori_loop(0, QUADS, left, 0)

    drain(GI.at[pl.ds(0, NZ - 1)], rsem.at[12])
    mine = pl.ds(pl.multiple_of(c * 64, 64), 64)
    gi_out[mine, :] = lax.fori_loop(1, NZ, lambda k, a: a + GI[k], GI[0], unroll=True)
    remote(gi_out.at[mine], gi_out.at[mine], ssem.at[13], rsem.at[13], sib).start()
    drain(YA.at[pl.ds(0, SIDE - 1)], rsem.at[48])
    gt_out[pl.ds(pl.multiple_of(c * 64, 64), 32), :] = total(YA)
    drain(XB.at[pl.ds(0, SIDE - 1)], rsem.at[50])
    gt_out[pl.ds(pl.multiple_of(c * 64 + 32, 32), 32), :] = total(XB)
    remote(gt_out.at[mine], gt_out.at[mine], ssem.at[14], rsem.at[14], sib).start()
    drain(gi_out.at[pl.ds(0, 64)], rsem.at[13])
    drain(gt_out.at[pl.ds(0, 64)], rsem.at[14])

    drain(XA.at[pl.ds(0, SIDE - 1)], ssem.at[6])
    drain(YA.at[pl.ds(0, SIDE - 1)], ssem.at[48])
    drain(YB.at[pl.ds(0, SIDE - 1)], ssem.at[49])
    drain(XB.at[pl.ds(0, SIDE - 1)], ssem.at[50])
    drain(GI.at[pl.ds(0, NZ - 1)], ssem.at[12])
    drain(gi_out.at[pl.ds(0, 64)], ssem.at[13])
    drain(gt_out.at[pl.ds(0, 64)], ssem.at[14])
    drain(GTR, ssem.at[15])


def run_exchange(x, y, pi, pt):
    pairs, dx = x.shape
    dy = y.shape[1]
    rank = 128
    iblock = dx // NZ
    half = iblock // 2
    lead = ZFIRST
    wide = half - lead
    vm = pltpu.VMEM
    scratch = [
        vm((pairs, dx), BF16), vm((pairs, dy), BF16),
        vm((iblock, rank), BF16), vm((128, rank), BF16),
        vm((NP, 2, 128, rank), BF16), vm((NZ, 2, half, rank), BF16),
        vm((pairs, rank), F32), vm((rank, pairs), BF16),
        vm((2, QUADS, NP, 16, wide), F32), vm((2, QUADS, NP, 16, wide), BF16),
        vm((QUADS, NP, 16, wide), BF16), vm((QUADS, NP, 16, wide), BF16),
        vm((QUADS, NP - 1, 16, wide), BF16),
        vm((2, NZ, rank, lead), F32), vm((2, NZ, rank, lead), BF16),
        vm((NZ, rank, lead), BF16), vm((NZ, rank, lead), BF16), vm((NZ, rank, lead), BF16),
        vm((NP, 8, lead), F32), vm((NP - 1, 8, lead), F32),
        vm((NZ, 8, wide), F32), vm((NZ - 1, 8, wide), F32), vm((8, half), F32),
        vm((NP, 8, half), F32), vm((NP, 8, half), F32),
        vm((2, NP, rank, 128), F32), vm((NP, rank, 128), F32),
        vm((NP, rank, 128), BF16), vm((NP - 1, rank, 128), BF16),
        vm((NZ, rank, 128), BF16),
        vm((NZ, 64, 128), F32), vm((rank, 128), F32), vm((2, 64, 128), F32), vm((64, 128), F32),
        vm((SIDE, 32, 128), F32), vm((SIDE, 32, 128), F32), vm((SIDE, 32, 128), F32), vm((SIDE, 32, 128), F32),
        pltpu.SemaphoreType.DMA((4,)), pltpu.SemaphoreType.DMA((51,)), pltpu.SemaphoreType.DMA((51,)),
    ]
    vspec = pl.BlockSpec(memory_space=pltpu.VMEM)
    aspec = pl.BlockSpec(memory_space=pl.ANY)
    square = jax.ShapeDtypeStruct((rank, rank), F32)
    return pl.pallas_call(
        exchange,
        out_shape=(jax.ShapeDtypeStruct((iblock, rank), F32), square, square, square),
        in_specs=[aspec] * 4,
        out_specs=(vspec,) * 4,
        scratch_shapes=scratch,
        name="panels",
        compiler_params=pltpu.CompilerParams(
            collective_id=0, has_side_effects=True, vmem_limit_bytes=60 << 20
        ),
        cost_estimate=pl.CostEstimate(
            flops=4 * pairs * (dx + dy) * rank, bytes_accessed=2 * pairs * (dx + dy), transcendentals=0
        ),
    )(x, y, pi, pt)


def lower_inverses(grams, outer=32):
    n = grams[0].shape[0]
    m = len(grams)
    lane8 = lax.broadcasted_iota(jnp.int32, (8, n), 1)
    sub8 = lax.broadcasted_iota(jnp.int32, (8, n), 0)
    lane = lax.broadcasted_iota(jnp.int32, (n, n), 1)
    laneo = lax.broadcasted_iota(jnp.int32, (outer, n), 1)
    subo = lax.broadcasted_iota(jnp.int32, (outer, n), 0)
    nv = outer // 8
    work = list(grams)
    done = [[] for _ in range(m)]
    for b in range(n // outer):
        j0 = b * outer
        R = [[w[j0 + 8 * v:j0 + 8 * v + 8, :] for v in range(nv)] for w in work]
        rec = [[None] * nv for _ in range(m)]
        scl = [[None] * nv for _ in range(m)]
        for s in range(nv):
            cols = [[[jnp.broadcast_to(R[t][v][:, j0 + 8 * s + k:j0 + 8 * s + k + 1], (8, n)) for v in range(nv)] if True else None
                     for k in range(8)] for t in range(m)]
            for t in range(m):
                rec[t][s] = jnp.zeros((8, n), F32); scl[t][s] = jnp.zeros((8, n), F32)
            for k in range(8):
                j = j0 + 8 * s + k
                for t in range(m):
                    piv = jnp.broadcast_to(cols[t][k][s][k:k + 1, :], (8, n))
                    inv = 1.0 / piv
                    rec[t][s] = jnp.where(sub8 == k, inv, rec[t][s])
                    scl[t][s] = jnp.where(sub8 == k, lax.rsqrt(piv), scl[t][s])
                    prow = jnp.where(lane8 == j, 1.0, jnp.broadcast_to(R[t][s][k:k + 1, :], (8, n)))
                    nxt = {q: jnp.broadcast_to(cols[t][q][s][k:k + 1, :], (8, n)) for q in range(k + 1, 8)}
                    for v in range(s, nv):
                        f = cols[t][k][v] * inv
                        hit = lane8 == j
                        if v == s:
                            f = jnp.where(sub8 > k, f, 0.0)
                            hit = hit & (sub8 >= k)
                            base = jnp.where(hit, jnp.where(sub8 == k, 1.0, 0.0), R[t][v])
                        else:
                            base = jnp.where(hit, 0.0, R[t][v])
                        R[t][v] = base - f * prow
                        for q in range(k + 1, 8):
                            cols[t][q][v] = cols[t][q][v] - f * nxt[q]
        for t in range(m):
            rows = jnp.concatenate(R[t], axis=0)
            inv = jnp.concatenate(rec[t], axis=0)
            scale = jnp.concatenate(scl[t], axis=0)
            done[t].append(jnp.where(laneo <= subo + j0, rows * scale, 0.0))
            if j0 + outer < n:
                right = laneo >= j0 + outer
                fac = jnp.where(right, rows * inv, 0.0)
                keep = jnp.where(right | (laneo <= subo + j0), rows, 0.0)
                upd = lax.dot_general(fac, keep, (((0,), (0,)), ((), ())), precision=HIGHEST, preferred_element_type=F32)
                work[t] = jnp.where((lane >= j0) & (lane < j0 + outer), 0.0, work[t]) - upd
    return [jnp.concatenate(d, axis=0) for d in done]

def product_nt(a, b):
    def split(v):
        high = v.astype(BF16)
        return high, (v - high.astype(F32)).astype(BF16)

    def dot(u, v):
        return lax.dot_general(u, v, (((1,), (1,)), ((), ())), preferred_element_type=F32)

    (ah, al), (bh, bl) = split(a), split(b)
    return dot(ah, bh) + (dot(ah, bl) + dot(al, bh))


def finish_kernel(
    img_hbm, txt_hbm, gi_ref, gt_ref, img_out, txt_out, img, txt, sem, *, image_width, text_width
):
    load_i = pltpu.make_async_copy(img_hbm, img, sem.at[0])
    load_t = pltpu.make_async_copy(txt_hbm, txt, sem.at[1])
    load_i.start()
    load_t.start()
    li, lt = lower_inverses([gi_ref[...], gt_ref[...]])
    load_i.wait()
    load_t.wait()
    img_out[...] = product_nt(img[...], li * math.sqrt(image_width))
    txt_out[...] = product_nt(txt[...], lt * math.sqrt(text_width))


def finish(img, txt, gi, gt, image_width, text_width):
    vspec = pl.BlockSpec(memory_space=pltpu.VMEM)
    aspec = pl.BlockSpec(memory_space=pl.ANY)
    return pl.pallas_call(
        functools.partial(finish_kernel, image_width=image_width, text_width=text_width),
        out_shape=(jax.ShapeDtypeStruct(img.shape, F32), jax.ShapeDtypeStruct(txt.shape, F32)),
        in_specs=[aspec, aspec, vspec, vspec],
        out_specs=(vspec, vspec),
        scratch_shapes=[
            pltpu.VMEM(img.shape, F32), pltpu.VMEM(txt.shape, F32), pltpu.SemaphoreType.DMA((2,))
        ],
        name="bases",
        compiler_params=pltpu.CompilerParams(vmem_limit_bytes=60 << 20),
    )(img, txt, gi, gt)


def per_device(image_feats, text_feats, probe_image, probe_text):
    img, txt, gi, gt = run_exchange(image_feats, text_feats, probe_image, probe_text)
    return finish(img, txt, gi, gt, image_feats.shape[1], text_feats.shape[1])


def solution(mesh):
    in_specs = (P(("row", "col"), None), P(("row", "col"), None), P("row", None), P("col", None))
    out_specs = (P("row", None), P("col", None))
    return jax.shard_map(
        per_device, mesh=mesh, in_specs=in_specs, out_specs=out_specs, check_vma=False
    )
```
